128 devices in a mesh: dp: 16 (over z, y_lo, core), mp: 8 (over x, y_hi).
Axes of the slice: x: 4, y: 4 (y_hi: 2, y_lo: 2; y = y_hi * 2 + y_lo), z: 4, core: 2. Of those that a mesh axis runs over, the one named last changes fastest.
Arguments:
- learn_hidden: bfloat16 [8192, 15360], P('dp', 'mp'), may hold values from -6 to 6
- out_cot: bfloat16 [8192, 4096], P('dp'), may hold values from -0.3125 to 0.3125
- master: float32 [15360, 4096], P(('mp', 'dp')), may hold values from -0.046875 to 0.046875
- moment_one: float32 [15360, 4096], P(('mp', 'dp')), may hold values from -4 to 4
- moment_two: float32 [15360, 4096], P(('mp', 'dp')), may hold values from 0.1 to 1
- queries: bfloat16 [4, 768, 4096], P(None, 'dp', 'mp'), may hold values from -100 to 100
- keys_cache: bfloat16 [768, 128, 1024], P('dp', None, 'mp'), may hold values from -5 to 5
- values_cache: bfloat16 [768, 128, 1024], P('dp', None, 'mp'), may hold values from -6 to 6
- keys_new: bfloat16 [4, 768, 1024], P(None, 'dp', 'mp'), may hold values from -6 to 6
- values_new: bfloat16 [4, 768, 1024], P(None, 'dp', 'mp'), may hold values from -6 to 6
- lengths: int32 [768], P('dp'), may hold values from 2 to 128
- residual: bfloat16 [4, 768, 4096], P(None, 'dp', 'mp'), may hold values from -50 to 50
- unit_acts: bfloat16 [4, 768, 8, 1920], P(None, 'dp', 'mp'), may hold values from -6 to 6
Outputs:
- mixed: bfloat16 [4, 768, 4096], P(None, 'dp', 'mp')
- master_next: float32 [15360, 4096], P(('mp', 'dp'))
- moment_one_next: float32 [15360, 4096], P(('mp', 'dp'))
- moment_two_next: float32 [15360, 4096], P(('mp', 'dp'))
The draws below stay inside these ranges and needn't reach their ends.
All inputs are finite; a program needn't handle non-finite values.
Results may differ from the reference program's by a relative error of at most 0.0095.
Values may be sent and summed in bfloat16 or wider, within the bound.
A program may use at most 128 MiB of HBM per device.

```python
import math
import jax
import jax.numpy as jnp
from jax import lax

D = 4096
HEADS = 32
KV_HEADS = 8
HEAD_DIM = 128
FFW = 15360
STEPS = 4
LEARN_TOK = 512
CACHE = 128
LEARN_ALL = 8192
ROWS_ALL = 768
N_DP = 16
N_MP = 8


def shared_keys(key):
    return jax.random.truncated_normal(jax.random.fold_in(key, 101), -4.0, 4.0, (ROWS_ALL, CACHE, KV_HEADS * HEAD_DIM), jnp.float32)


def draw_keys_cache(key, part):
    key_draw = shared_keys(key)
    return key_draw.astype(jnp.bfloat16)


def draw_queries(key, part):
    key = jax.random.fold_in(key, 13)
    drawn = jax.random.truncated_normal(key, -4.0, 4.0, (STEPS, ROWS_ALL, HEADS * HEAD_DIM), jnp.float32)
    return drawn.astype(jnp.bfloat16)


def draw_residual(key, part):
    key = jax.random.fold_in(key, 29)
    subkeys = jax.random.split(key, 3)
    drawn = jax.random.truncated_normal(subkeys[0], -4.0, 4.0, (STEPS, ROWS_ALL, D), jnp.float32)
    col_low, col_high, row_low, row_high = (0.4, 4.0, 0.5, 2.0)
    col_scale = jnp.exp(jax.random.uniform(subkeys[1], (D,), jnp.float32, jnp.log(col_low), jnp.log(col_high)))
    row_scale = jnp.exp(jax.random.uniform(subkeys[2], (STEPS, ROWS_ALL, 1), jnp.float32, jnp.log(row_low), jnp.log(row_high)))
    return (drawn * col_scale * row_scale).astype(jnp.bfloat16)


def touch_ends(result, rng, least, largest):
    place = [jax.random.randint(jax.random.fold_in(rng, axis), (), 0, length) for axis, length in enumerate(result.shape)]
    main_axis = result.shape.index(max(result.shape))
    next_to = place[:main_axis] + [(place[main_axis] + 1) % result.shape[main_axis]] + place[main_axis + 1:]
    return result.at[tuple(place)].set(least).at[tuple(next_to)].set(largest)


def steps_of(own_key, shape, cuts, least, high):
    factor_of = 1.0
    for dim, parts in cuts:
        steps = jax.random.uniform(jax.random.fold_in(jax.random.fold_in(own_key, 6), dim), (parts,), jnp.float32, least / len(cuts), high / len(cuts))
        factor_of = factor_of * jnp.repeat(jnp.exp(steps), shape[dim] // parts).reshape((-1,) + (1,) * (len(shape) - 1 - dim))
    return factor_of


def scatter_about(key, extent, spread, limit, pieces=(), held_as=jnp.bfloat16):
    result = jax.random.normal(key, extent, jnp.float32) * spread
    if len(pieces) > 0:
        result = steps_of(key, extent, pieces, -0.22, 0.18) * result
    return jnp.clip(result, min=-limit, max=limit).astype(held_as)


def setup_inputs(seed: int = 0) -> dict:
    seeds = jax.random.split(jax.random.key(seed), 14)
    learn_hidden = scatter_about(seeds[0], (LEARN_ALL, FFW), 1.0, 6.0, ((0, 16), (1, 8)))
    out_cot = scatter_about(seeds[1], (LEARN_ALL, D), 0.02, 0.3125, ((0, 16),))
    master = scatter_about(seeds[2], (FFW, D), FFW ** -0.5, 0.046875, ((0, 128),), jnp.float32)
    moment_one = scatter_about(seeds[3], (FFW, D), 0.5, 4.0, ((0, 128),), jnp.float32)
    moment_two = jnp.clip(jnp.exp(math.log(1.0) - 2.3025851 * jax.random.uniform(seeds[4], (FFW, D), jnp.float32) ** steps_of(seeds[4], (FFW, D), ((0, 128),), -0.2, 0.2)), 0.1, 1.0)
    queries = draw_queries(jax.random.fold_in(seeds[13], 71), 0)
    keys_cache = draw_keys_cache(jax.random.fold_in(seeds[13], 71), 0)
    values_cache = scatter_about(seeds[7], (ROWS_ALL, CACHE, KV_HEADS * HEAD_DIM), 1.0, 6.0, ((0, 16), (2, 8)))
    keys_new = scatter_about(seeds[8], (STEPS, ROWS_ALL, KV_HEADS * HEAD_DIM), 1.0, 6.0, ((1, 16), (2, 8)))
    values_new = scatter_about(seeds[9], (STEPS, ROWS_ALL, KV_HEADS * HEAD_DIM), 1.0, 6.0, ((1, 16), (2, 8)))
    lengths = touch_ends(jax.random.randint(seeds[10], (ROWS_ALL,), 2, CACHE + 1), jax.random.fold_in(seeds[10], 1), 2, CACHE).astype(jnp.int32)
    residual = draw_residual(jax.random.fold_in(seeds[13], 71), 0)
    unit_acts = scatter_about(seeds[12], (STEPS, ROWS_ALL, N_MP, FFW // N_MP), 1.0, 6.0, ((1, 16), (2, 8)))
    return {"learn_hidden": learn_hidden, "out_cot": out_cot, "master": master, "moment_one": moment_one, "moment_two": moment_two, "queries": queries, "keys_cache": keys_cache, "values_cache": values_cache, "keys_new": keys_new, "values_new": values_new, "lengths": lengths, "residual": residual, "unit_acts": unit_acts}


beta_one = 0.9
beta_two = 0.999
learn_rate = 0.01
decay_rate = 0.1
adam_eps = 1e-08
bias_steps = 10.0

def gradient(learn_hidden, out_cot):
    blocks = (learn_hidden.reshape(N_DP, LEARN_TOK, FFW), out_cot.reshape(N_DP, LEARN_TOK, D))

    def accumulate(running, portion):
        hidden_acts, out_part = portion
        block_term = jnp.dot(hidden_acts.T, out_part, preferred_element_type=jnp.float32)
        rounded = lax.optimization_barrier(block_term.astype(jnp.bfloat16))
        return (running + rounded.astype(jnp.float32), None)
    running, unused = lax.scan(accumulate, jnp.zeros((FFW, D), jnp.float32), blocks)
    return running

def attend(queries, keys_cache, values_cache, keys_new, values_new, lengths):
    step_count, row_count, row_width = queries.shape
    cache_len = keys_cache.shape[1]
    per_group = HEADS // KV_HEADS
    query_heads = queries.astype(jnp.float32).reshape(step_count, row_count, KV_HEADS, per_group, HEAD_DIM)
    cache_keys = keys_cache.astype(jnp.float32).reshape(row_count, cache_len, KV_HEADS, HEAD_DIM)
    cache_values = values_cache.astype(jnp.float32).reshape(row_count, cache_len, KV_HEADS, HEAD_DIM)
    new_keys = keys_new.astype(jnp.float32).reshape(step_count, row_count, KV_HEADS, HEAD_DIM)
    new_values = values_new.astype(jnp.float32).reshape(step_count, row_count, KV_HEADS, HEAD_DIM)
    score_scale = HEAD_DIM ** (-0.5)
    cache_scores = jnp.einsum('trkgd,rlkd->trkgl', query_heads, cache_keys) * score_scale
    new_scores = jnp.einsum('trkgd,srkd->trkgs', query_heads, new_keys) * score_scale
    visible = jnp.arange(cache_len)[None, :] < lengths[:, None]
    causal = jnp.arange(step_count)[:, None] >= jnp.arange(step_count)[None, :]
    cache_scores = jnp.where(visible[None, :, None, None, :], cache_scores, -jnp.inf)
    new_scores = jnp.where(causal[:, None, None, None, :], new_scores, -jnp.inf)
    highest = jnp.maximum(lax.optimization_barrier(jnp.max(cache_scores, axis=-1)), lax.optimization_barrier(jnp.max(new_scores, axis=-1)))
    cache_exp = jnp.exp(cache_scores - highest[..., None])
    new_exp = jnp.exp(new_scores - highest[..., None])
    exp_total = lax.optimization_barrier(jnp.sum(cache_exp, axis=-1)) + lax.optimization_barrier(jnp.sum(new_exp, axis=-1))
    cache_probs = (cache_exp / exp_total[..., None]).astype(jnp.bfloat16).astype(jnp.float32)
    new_probs = (new_exp / exp_total[..., None]).astype(jnp.bfloat16).astype(jnp.float32)
    mixed_heads = jnp.einsum('trkgl,rlkd->trkgd', cache_probs, cache_values)
    mixed_heads = mixed_heads + jnp.einsum('trkgs,srkd->trkgd', new_probs, new_values)
    return mixed_heads.reshape(step_count, row_count, row_width).astype(jnp.bfloat16)

def reference(learn_hidden, out_cot, master, moment_one, moment_two, queries, keys_cache, values_cache, keys_new, values_new, lengths, residual, unit_acts):
    grad_rows = gradient(learn_hidden, out_cot)
    moment_one_next = beta_one * moment_one + (1.0 - beta_one) * grad_rows
    moment_two_next = beta_two * moment_two + (1.0 - beta_two) * grad_rows * grad_rows
    first_hat = moment_one_next / (1.0 - beta_one ** bias_steps)
    second_hat = moment_two_next / (1.0 - beta_two ** bias_steps)
    master_next = master - learn_rate * (first_hat / (jnp.sqrt(second_hat) + adam_eps) + decay_rate * master)
    fresh_rows = master_next.astype(jnp.bfloat16)
    attended = attend(queries, keys_cache, values_cache, keys_new, values_new, lengths)
    stream = (residual.astype(jnp.float32) + attended.astype(jnp.float32)).astype(jnp.bfloat16)
    stream_f = stream.astype(jnp.float32)
    flat_acts = jnp.swapaxes(unit_acts, 2, 3).reshape(-1, FFW)
    ffn_out = jnp.dot(flat_acts, fresh_rows, preferred_element_type=jnp.float32)
    mixed = (stream_f + ffn_out.reshape(stream.shape)).astype(jnp.bfloat16)
    return (mixed, master_next, moment_one_next, moment_two_next)
```

```python
import functools
import jax
import jax.numpy as jnp
from jax import lax
from jax.experimental import pallas as pl
from jax.experimental.pallas import tpu as pltpu
from jax.sharding import PartitionSpec as P

MESHID = pl.DeviceIdType.MESH
bf16, f32 = jnp.bfloat16, jnp.float32
NZ = 5
NY = 3
W = 256
HW = W // 2


def coords():
    dp, mp = lax.axis_index("dp"), lax.axis_index("mp")
    return dp // 4, (dp // 2) % 2, dp % 2, mp // 2, mp % 2


def place(z, y_lo, core, x, y_hi):
    return ((z * 2 + y_lo) * 2 + core, x * 2 + y_hi)


def grad_kernel(ht, cot, out, hs, cs, zs1, zsb, zs2, zr1, zrb, zr2, zhold, zown, zys, zyr,
                yys, yyr, ys1, ysb, ys2, yr1, yrb, yr2, yhold, yown, gbuf,
                in_sem, send_sem, recv_sem):
    z, y_lo, core, x, y_hi = coords()
    sib = place(z, y_lo, 1 - core, x, y_hi)
    up = place((z + 1) % 4, y_lo, core, x, y_hi)
    down = place((z + 3) % 4, y_lo, core, x, y_hi)
    across = place(z, 1 - y_lo, core, x, y_hi)

    barrier = pltpu.get_barrier_semaphore()
    for other in (sib, up, down, across):
        pl.semaphore_signal(barrier, inc=1, device_id=other, device_id_type=MESHID)
    pl.semaphore_wait(barrier, 4)

    count = [0]
    sends = []

    def send(src, dst, device):
        i = count[0]
        count[0] += 1
        copy = pltpu.make_async_remote_copy(
            src_ref=src, dst_ref=dst, send_sem=send_sem.at[i], recv_sem=recv_sem.at[i],
            device_id=device, device_id_type=MESHID)
        copy.start()
        sends.append(copy)
        return copy

    chunks = NZ + NY
    order = [0, 5, 1, 6, 2, 7, 3, 4]
    h_own = pltpu.make_async_copy(ht, hs.at[:, :, pl.ds(0, 512)], in_sem.at[chunks])
    h_own.start()
    h_sib = send(ht, hs.at[:, :, pl.ds(512, 512)], sib)
    c_own, c_sib = {}, {}
    for j in order:
        mine = pl.ds(pl.multiple_of(core * 2048 + j * W, W), W)
        theirs = pl.ds(pl.multiple_of((1 - core) * 2048 + j * W, W), W)
        c_own[j] = pltpu.make_async_copy(cot.at[:, mine], cs.at[j, pl.ds(0, 512)], in_sem.at[j])
        c_own[j].start()
        c_sib[j] = send(cot.at[:, theirs], cs.at[j, pl.ds(512, 512)], sib)
    h_own.wait()
    h_sib.wait_recv()

    def ready(j):
        c_own[j].wait()
        c_sib[j].wait_recv()

    def rows480(zb, j):
        lhs = hs[pl.ds(2 * zb, 2)].reshape(480, 1024)
        return jnp.dot(lhs, cs[j], preferred_element_type=f32)

    def rows240(zb, yb, j):
        return jnp.dot(hs[2 * zb + yb], cs[j], preferred_element_type=f32)

    zp, zm, zf = (z + 1) % 4, (z + 3) % 4, (z + 2) % 4
    state = {}

    def ring_start(key, term, s1, sb, r1, rb, hold, own):
        p = term(zf)
        s1[0] = p[:, :HW].astype(bf16)
        s1[1] = p[:, HW:].astype(bf16)
        st = {"r1": [send(s1.at[0], r1.at[0], up), send(s1.at[1], r1.at[1], down)]}
        p = term(zp)
        sb[0] = p[:, HW:].astype(bf16)
        b0 = send(sb.at[0], rb.at[0], up)
        hold[0] = p[:, :HW]
        p = term(zm)
        sb[1] = p[:, :HW].astype(bf16)
        b1 = send(sb.at[1], rb.at[1], down)
        hold[1] = p[:, HW:]
        st["rb"] = [b0, b1]
        own[...] = term(z)
        state[key] = st

    def ring_mid(key, s2, r1, r2, hold):
        st = state[key]
        st["r2"] = []
        for d, device in ((0, up), (1, down)):
            st["r1"][d].wait_recv()
            s2[d] = (hold[d] + r1[d].astype(f32)).astype(bf16)
            st["r2"].append(send(s2.at[d], r2.at[d], device))

    def ring_end(key, rb, r2, own):
        st = state[key]
        st["rb"][1].wait_recv()
        st["r2"][0].wait_recv()
        left = own[:, :HW] + rb[1].astype(f32) + r2[0].astype(f32)
        st["rb"][0].wait_recv()
        st["r2"][1].wait_recv()
        right = own[:, HW:] + rb[0].astype(f32) + r2[1].astype(f32)
        return left, right

    gsend = []

    def finish(j, left, right):
        gbuf[j, :, :, pl.ds(0, HW)] = left.reshape(2, 120, HW)
        gbuf[j, :, :, pl.ds(HW, HW)] = right.reshape(2, 120, HW)
        cols = pl.ds(pl.multiple_of(core * 2048 + j * W, W), W)
        gsend.append(send(gbuf.at[j, 1 - core], out.at[:, cols], sib))
        out[:, cols] = gbuf[j, core]

    def zc(k):
        ready(k)
        ring_start(("z", k), lambda zb: rows480(zb, k), zs1.at[k], zsb.at[k], zr1.at[k], zrb.at[k], zhold.at[k], zown.at[k])

    def zm_(k):
        ring_mid(("z", k), zs2.at[k], zr1.at[k], zr2.at[k], zhold.at[k])

    def ze(k):
        left, right = ring_end(("z", k), zrb.at[k], zr2.at[k], zown.at[k])
        zown[k, :, pl.ds(0, HW)] = left
        zown[k, :, pl.ds(HW, HW)] = right
        theirs = pl.ds(pl.multiple_of((1 - y_lo) * 240, 16), 240)
        zys[k] = zown[k, theirs, :].astype(bf16)
        state[("zy", k)] = send(zys.at[k], zyr.at[k], across)

    def zf_(k):
        state[("zy", k)].wait_recv()
        mine = pl.ds(pl.multiple_of(y_lo * 240, 16), 240)
        total = zown[k, mine, :] + zyr[k].astype(f32)
        finish(k, total[:, :HW], total[:, HW:])

    def yc(k):
        j = NZ + k
        ready(j)
        def body(zb, carry):
            yys[k, zb] = rows240(zb, 1 - y_lo, j).astype(bf16)
            return carry
        lax.fori_loop(0, 4, body, 0)
        state[("yy", k)] = send(yys.at[k], yyr.at[k], across)

    def ys(k):
        j = NZ + k
        state[("yy", k)].wait_recv()
        ring_start(("y", k), lambda zb: rows240(zb, y_lo, j) + yyr[k, zb].astype(f32),
                   ys1.at[k], ysb.at[k], yr1.at[k], yrb.at[k], yhold.at[k], yown.at[k])

    def ym(k):
        ring_mid(("y", k), ys2.at[k], yr1.at[k], yr2.at[k], yhold.at[k])

    def ye(k):
        left, right = ring_end(("y", k), yrb.at[k], yr2.at[k], yown.at[k])
        finish(NZ + k, left, right)

    zc(0); yc(0); zc(1); yc(1); zm_(0); yc(2); zc(2); zm_(1); ys(0); ze(0); zc(3); zm_(2); ze(1); ym(0); ys(1)
    zc(4); zm_(3); ze(2); ym(1); ye(0); ys(2); zf_(0); zm_(4); ze(3); zf_(1); ym(2); ye(1); zf_(2); ze(4); zf_(3); ye(2); zf_(4)

    for copy in gsend:
        copy.wait_recv()
    for copy in sends:
        copy.wait_send()


def grad_sum(learn_hidden, out_cot):
    ht = learn_hidden.T.reshape(8, 240, 512)
    ring = lambda n, r: [pltpu.VMEM((n, 2, r, HW), bf16)] * 6 + [pltpu.VMEM((n, 2, r, HW), f32), pltpu.VMEM((n, r, W), f32)]
    copies = 1 + 8 + NZ * 8 + NY * 8
    return pl.pallas_call(
        grad_kernel,
        out_shape=jax.ShapeDtypeStruct((120, 4096), f32),
        in_specs=[pl.BlockSpec(memory_space=pl.ANY)] * 2,
        out_specs=pl.BlockSpec(memory_space=pltpu.VMEM),
        scratch_shapes=[
            pltpu.VMEM((8, 240, 1024), bf16),
            pltpu.VMEM((NZ + NY, 1024, W), bf16),
            *ring(NZ, 480),
            pltpu.VMEM((NZ, 240, W), bf16),
            pltpu.VMEM((NZ, 240, W), bf16),
            pltpu.VMEM((NY, 4, 240, W), bf16),
            pltpu.VMEM((NY, 4, 240, W), bf16),
            *ring(NY, 240),
            pltpu.VMEM((NZ + NY, 2, 120, W), f32),
            pltpu.SemaphoreType.DMA((NZ + NY + 1,)),
            pltpu.SemaphoreType.DMA((copies,)),
            pltpu.SemaphoreType.DMA((copies,)),
        ],
        compiler_params=pltpu.CompilerParams(collective_id=0, has_side_effects=True, vmem_limit_bytes=52 * 2**20),
        cost_estimate=pl.CostEstimate(flops=8053063680, bytes_accessed=8 * 2**20, transcendentals=0),
        name="gradient_sum",
    )(ht, out_cot)


HEADS = 32
KV_HEADS = 8
HEAD_DIM = 128


beta_one = 0.9
beta_two = 0.999
learn_rate = 0.01
decay_rate = 0.1
adam_eps = 1e-08
bias_steps = 10.0


def attend(queries, keys_cache, values_cache, keys_new, values_new, lengths):
    step_count, row_count, row_width = queries.shape
    cache_len = keys_cache.shape[1]
    kv_local = keys_cache.shape[2] // HEAD_DIM
    per_group = HEADS // KV_HEADS
    query_heads = queries.reshape(step_count, row_count, kv_local, per_group, HEAD_DIM)
    cache_keys = keys_cache.reshape(row_count, cache_len, kv_local, HEAD_DIM)
    cache_values = values_cache.reshape(row_count, cache_len, kv_local, HEAD_DIM)
    new_keys = keys_new.reshape(step_count, row_count, kv_local, HEAD_DIM)
    new_values = values_new.reshape(step_count, row_count, kv_local, HEAD_DIM)
    score_scale = HEAD_DIM ** (-0.5)
    cache_scores = (
        jnp.einsum("trkgd,rlkd->trkgl", query_heads, cache_keys, preferred_element_type=jnp.float32)
        * score_scale
    )
    new_scores = (
        jnp.einsum("trkgd,srkd->trkgs", query_heads, new_keys, preferred_element_type=jnp.float32)
        * score_scale
    )
    visible = jnp.arange(cache_len)[None, :] < lengths[:, None]
    causal = jnp.arange(step_count)[:, None] >= jnp.arange(step_count)[None, :]
    cache_scores = jnp.where(visible[None, :, None, None, :], cache_scores, -jnp.inf)
    new_scores = jnp.where(causal[:, None, None, None, :], new_scores, -jnp.inf)
    highest = jnp.maximum(jnp.max(cache_scores, axis=-1), jnp.max(new_scores, axis=-1))
    cache_exp = jnp.exp(cache_scores - highest[..., None])
    new_exp = jnp.exp(new_scores - highest[..., None])
    exp_total = jnp.sum(cache_exp, axis=-1) + jnp.sum(new_exp, axis=-1)
    cache_probs = (cache_exp / exp_total[..., None]).astype(jnp.bfloat16)
    new_probs = (new_exp / exp_total[..., None]).astype(jnp.bfloat16)
    mixed_heads = jnp.einsum(
        "trkgl,rlkd->trkgd", cache_probs, cache_values, preferred_element_type=jnp.float32
    )
    mixed_heads = mixed_heads + jnp.einsum(
        "trkgs,srkd->trkgd", new_probs, new_values, preferred_element_type=jnp.float32
    )
    return mixed_heads.reshape(step_count, row_count, row_width).astype(jnp.bfloat16)


def make_adder(acts_view, portion):
    return jnp.einsum("amc,cmd->ad", acts_view, portion, preferred_element_type=jnp.float32)


def local(
    learn_hidden,
    out_cot,
    master,
    moment_one,
    moment_two,
    queries,
    keys_cache,
    values_cache,
    keys_new,
    values_new,
    lengths,
    residual,
    unit_acts,
):
    gradient_rows = grad_sum(learn_hidden, out_cot)
    moment_one_next = beta_one * moment_one + (1.0 - beta_one) * gradient_rows
    moment_two_next = beta_two * moment_two + (1.0 - beta_two) * gradient_rows * gradient_rows
    first_hat = moment_one_next / (1.0 - beta_one**bias_steps)
    second_hat = moment_two_next / (1.0 - beta_two**bias_steps)
    master_next = master - learn_rate * (
        first_hat / (jnp.sqrt(second_hat) + adam_eps) + decay_rate * master
    )
    fresh_rows = master_next.astype(jnp.bfloat16)
    attended = attend(queries, keys_cache, values_cache, keys_new, values_new, lengths)
    stream = (residual.astype(jnp.float32) + attended.astype(jnp.float32)).astype(jnp.bfloat16)
    step_count, row_count, share_width = stream.shape
    unit_local = unit_acts.shape[3]
    width = fresh_rows.shape[1]
    mp_count = lax.axis_size("mp")
    own_rows = fresh_rows.shape[0]
    spread = fresh_rows.reshape(own_rows // mp_count, mp_count, width)
    unit_pieces = lax.all_to_all(spread, "mp", split_axis=1, concat_axis=1, tiled=True)
    acts_view = unit_acts.reshape(step_count * row_count, mp_count, unit_local // mp_count)
    running = make_adder(acts_view, lax.all_gather(unit_pieces, "dp", axis=0, tiled=True))
    partials = running.reshape(step_count, row_count, width)
    summed = lax.psum_scatter(
        partials.astype(jnp.bfloat16), "mp", scatter_dimension=2, tiled=True
    ).astype(jnp.float32)
    mixed = (stream.astype(jnp.float32) + summed).astype(jnp.bfloat16)
    return (mixed, master_next, moment_one_next, moment_two_next)


def solution(mesh):
    placed = (
        P("dp", "mp"),
        P("dp", None),
        P(("mp", "dp"), None),
        P(("mp", "dp"), None),
        P(("mp", "dp"), None),
        P(None, "dp", "mp"),
        P("dp", None, "mp"),
        P("dp", None, "mp"),
        P(None, "dp", "mp"),
        P(None, "dp", "mp"),
        P("dp"),
        P(None, "dp", "mp"),
        P(None, "dp", "mp", None),
    )
    return jax.shard_map(
        local,
        mesh=mesh,
        in_specs=placed,
        out_specs=(
            P(None, "dp", "mp"),
            P(("mp", "dp"), None),
            P(("mp", "dp"), None),
            P(("mp", "dp"), None),
        ),
        check_vma=False,
    )
```

```python
import functools
import jax
import jax.numpy as jnp
from jax import lax
from jax.experimental import pallas as pl
from jax.experimental.pallas import tpu as pltpu
from jax.sharding import PartitionSpec as P

MESHID = pl.DeviceIdType.MESH
bf16, f32 = jnp.bfloat16, jnp.float32
NZ = 5
NY = 3
W = 256
HW = W // 2


def coords():
    dp, mp = lax.axis_index("dp"), lax.axis_index("mp")
    return dp // 4, (dp // 2) % 2, dp % 2, mp // 2, mp % 2


def place(z, y_lo, core, x, y_hi):
    return ((z * 2 + y_lo) * 2 + core, x * 2 + y_hi)


def grad_kernel(ht, cot, out, hs, cs, zs1, zsb, zs2, zr1, zrb, zr2, zhold, zown, zys, zyr,
                yys, yyr, ys1, ysb, ys2, yr1, yrb, yr2, yhold, yown, gbuf,
                in_sem, send_sem, recv_sem):
    z, y_lo, core, x, y_hi = coords()
    sib = place(z, y_lo, 1 - core, x, y_hi)
    up = place((z + 1) % 4, y_lo, core, x, y_hi)
    down = place((z + 3) % 4, y_lo, core, x, y_hi)
    across = place(z, 1 - y_lo, core, x, y_hi)

    barrier = pltpu.get_barrier_semaphore()
    for other in (sib, up, down, across):
        pl.semaphore_signal(barrier, inc=1, device_id=other, device_id_type=MESHID)
    pl.semaphore_wait(barrier, 4)

    count = [0]
    sends = []

    def send(src, dst, device):
        i = count[0]
        count[0] += 1
        copy = pltpu.make_async_remote_copy(
            src_ref=src, dst_ref=dst, send_sem=send_sem.at[i], recv_sem=recv_sem.at[i],
            device_id=device, device_id_type=MESHID)
        copy.start()
        sends.append(copy)
        return copy

    chunks = NZ + NY
    order = [0, 5, 1, 6, 2, 7, 3, 4]
    h_own = pltpu.make_async_copy(ht, hs.at[:, :, pl.ds(0, 512)], in_sem.at[chunks])
    h_own.start()
    h_sib = send(ht, hs.at[:, :, pl.ds(512, 512)], sib)
    c_own, c_sib = {}, {}
    for j in order:
        mine = pl.ds(pl.multiple_of(core * 2048 + j * W, W), W)
        theirs = pl.ds(pl.multiple_of((1 - core) * 2048 + j * W, W), W)
        c_own[j] = pltpu.make_async_copy(cot.at[:, mine], cs.at[j, pl.ds(0, 512)], in_sem.at[j])
        c_own[j].start()
        c_sib[j] = send(cot.at[:, theirs], cs.at[j, pl.ds(512, 512)], sib)
    h_own.wait()
    h_sib.wait_recv()

    def ready(j):
        c_own[j].wait()
        c_sib[j].wait_recv()

    def rows480(zb, j):
        lhs = hs[pl.ds(2 * zb, 2)].reshape(480, 1024)
        return jnp.dot(lhs, cs[j], preferred_element_type=f32)

    def rows240(zb, yb, j):
        return jnp.dot(hs[2 * zb + yb], cs[j], preferred_element_type=f32)

    zp, zm, zf = (z + 1) % 4, (z + 3) % 4, (z + 2) % 4
    state = {}

    def ring_start(key, term, s1, sb, r1, rb, hold, own):
        p = term(zf)
        s1[0] = p[:, :HW].astype(bf16)
        s1[1] = p[:, HW:].astype(bf16)
        st = {"r1": [send(s1.at[0], r1.at[0], up), send(s1.at[1], r1.at[1], down)]}
        p = term(zp)
        sb[0] = p[:, HW:].astype(bf16)
        b0 = send(sb.at[0], rb.at[0], up)
        hold[0] = p[:, :HW]
        p = term(zm)
        sb[1] = p[:, :HW].astype(bf16)
        b1 = send(sb.at[1], rb.at[1], down)
        hold[1] = p[:, HW:]
        st["rb"] = [b0, b1]
        own[...] = term(z)
        state[key] = st

    def ring_mid(key, s2, r1, r2, hold):
        st = state[key]
        st["r2"] = []
        for d, device in ((0, up), (1, down)):
            st["r1"][d].wait_recv()
            s2[d] = (hold[d] + r1[d].astype(f32)).astype(bf16)
            st["r2"].append(send(s2.at[d], r2.at[d], device))

    def ring_end(key, rb, r2, own):
        st = state[key]
        st["rb"][1].wait_recv()
        st["r2"][0].wait_recv()
        left = own[:, :HW] + rb[1].astype(f32) + r2[0].astype(f32)
        st["rb"][0].wait_recv()
        st["r2"][1].wait_recv()
        right = own[:, HW:] + rb[0].astype(f32) + r2[1].astype(f32)
        return left, right

    gsend = []

    def finish(j, left, right):
        gbuf[j, :, :, pl.ds(0, HW)] = left.reshape(2, 120, HW)
        gbuf[j, :, :, pl.ds(HW, HW)] = right.reshape(2, 120, HW)
        cols = pl.ds(pl.multiple_of(core * 2048 + j * W, W), W)
        gsend.append(send(gbuf.at[j, 1 - core], out.at[:, cols], sib))
        out[:, cols] = gbuf[j, core]

    def zc(k):
        ready(k)
        ring_start(("z", k), lambda zb: rows480(zb, k), zs1.at[k], zsb.at[k], zr1.at[k], zrb.at[k], zhold.at[k], zown.at[k])

    def zm_(k):
        ring_mid(("z", k), zs2.at[k], zr1.at[k], zr2.at[k], zhold.at[k])

    def ze(k):
        left, right = ring_end(("z", k), zrb.at[k], zr2.at[k], zown.at[k])
        zown[k, :, pl.ds(0, HW)] = left
        zown[k, :, pl.ds(HW, HW)] = right
        theirs = pl.ds(pl.multiple_of((1 - y_lo) * 240, 16), 240)
        zys[k] = zown[k, theirs, :].astype(bf16)
        state[("zy", k)] = send(zys.at[k], zyr.at[k], across)

    def zf_(k):
        state[("zy", k)].wait_recv()
        mine = pl.ds(pl.multiple_of(y_lo * 240, 16), 240)
        total = zown[k, mine, :] + zyr[k].astype(f32)
        finish(k, total[:, :HW], total[:, HW:])

    def yc(k):
        j = NZ + k
        ready(j)
        def body(zb, carry):
            yys[k, zb] = rows240(zb, 1 - y_lo, j).astype(bf16)
            return carry
        lax.fori_loop(0, 4, body, 0)
        state[("yy", k)] = send(yys.at[k], yyr.at[k], across)

    def ys(k):
        j = NZ + k
        state[("yy", k)].wait_recv()
        ring_start(("y", k), lambda zb: rows240(zb, y_lo, j) + yyr[k, zb].astype(f32),
                   ys1.at[k], ysb.at[k], yr1.at[k], yrb.at[k], yhold.at[k], yown.at[k])

    def ym(k):
        ring_mid(("y", k), ys2.at[k], yr1.at[k], yr2.at[k], yhold.at[k])

    def ye(k):
        left, right = ring_end(("y", k), yrb.at[k], yr2.at[k], yown.at[k])
        finish(NZ + k, left, right)

    zc(0); yc(0); zc(1); yc(1); zm_(0); yc(2); zc(2); zm_(1); ys(0); ze(0); zc(3); zm_(2); ze(1); ym(0); ys(1)
    zc(4); zm_(3); ze(2); ym(1); ye(0); ys(2); zf_(0); zm_(4); ze(3); zf_(1); ym(2); ye(1); zf_(2); ze(4); zf_(3); ye(2); zf_(4)

    for copy in gsend:
        copy.wait_recv()
    for copy in sends:
        copy.wait_send()


def grad_sum(learn_hidden, out_cot):
    ht = learn_hidden.T.reshape(8, 240, 512)
    ring = lambda n, r: [pltpu.VMEM((n, 2, r, HW), bf16)] * 6 + [pltpu.VMEM((n, 2, r, HW), f32), pltpu.VMEM((n, r, W), f32)]
    copies = 1 + 8 + NZ * 8 + NY * 8
    return pl.pallas_call(
        grad_kernel,
        out_shape=jax.ShapeDtypeStruct((120, 4096), f32),
        in_specs=[pl.BlockSpec(memory_space=pl.ANY)] * 2,
        out_specs=pl.BlockSpec(memory_space=pltpu.VMEM),
        scratch_shapes=[
            pltpu.VMEM((8, 240, 1024), bf16),
            pltpu.VMEM((NZ + NY, 1024, W), bf16),
            *ring(NZ, 480),
            pltpu.VMEM((NZ, 240, W), bf16),
            pltpu.VMEM((NZ, 240, W), bf16),
            pltpu.VMEM((NY, 4, 240, W), bf16),
            pltpu.VMEM((NY, 4, 240, W), bf16),
            *ring(NY, 240),
            pltpu.VMEM((NZ + NY, 2, 120, W), f32),
            pltpu.SemaphoreType.DMA((NZ + NY + 1,)),
            pltpu.SemaphoreType.DMA((copies,)),
            pltpu.SemaphoreType.DMA((copies,)),
        ],
        compiler_params=pltpu.CompilerParams(collective_id=0, has_side_effects=True, vmem_limit_bytes=52 * 2**20),
        cost_estimate=pl.CostEstimate(flops=8053063680, bytes_accessed=8 * 2**20, transcendentals=0),
        name="gradient_sum",
    )(ht, out_cot)


HEADS = 32
KV_HEADS = 8
HEAD_DIM = 128


beta_one = 0.9
beta_two = 0.999
learn_rate = 0.01
decay_rate = 0.1
adam_eps = 1e-08
bias_steps = 10.0


def attend(queries, keys_cache, values_cache, keys_new, values_new, lengths):
    step_count, row_count, row_width = queries.shape
    cache_len = keys_cache.shape[1]
    kv_local = keys_cache.shape[2] // HEAD_DIM
    per_group = HEADS // KV_HEADS
    query_heads = queries.reshape(step_count, row_count, kv_local, per_group, HEAD_DIM)
    cache_keys = keys_cache.reshape(row_count, cache_len, kv_local, HEAD_DIM)
    cache_values = values_cache.reshape(row_count, cache_len, kv_local, HEAD_DIM)
    new_keys = keys_new.reshape(step_count, row_count, kv_local, HEAD_DIM)
    new_values = values_new.reshape(step_count, row_count, kv_local, HEAD_DIM)
    score_scale = HEAD_DIM ** (-0.5)
    cache_scores = (
        jnp.einsum("trkgd,rlkd->trkgl", query_heads, cache_keys, preferred_element_type=jnp.float32)
        * score_scale
    )
    new_scores = (
        jnp.einsum("trkgd,srkd->trkgs", query_heads, new_keys, preferred_element_type=jnp.float32)
        * score_scale
    )
    visible = jnp.arange(cache_len)[None, :] < lengths[:, None]
    causal = jnp.arange(step_count)[:, None] >= jnp.arange(step_count)[None, :]
    cache_scores = jnp.where(visible[None, :, None, None, :], cache_scores, -jnp.inf)
    new_scores = jnp.where(causal[:, None, None, None, :], new_scores, -jnp.inf)
    highest = jnp.maximum(jnp.max(cache_scores, axis=-1), jnp.max(new_scores, axis=-1))
    cache_exp = jnp.exp(cache_scores - highest[..., None])
    new_exp = jnp.exp(new_scores - highest[..., None])
    exp_total = jnp.sum(cache_exp, axis=-1) + jnp.sum(new_exp, axis=-1)
    cache_probs = (cache_exp / exp_total[..., None]).astype(jnp.bfloat16)
    new_probs = (new_exp / exp_total[..., None]).astype(jnp.bfloat16)
    mixed_heads = jnp.einsum(
        "trkgl,rlkd->trkgd", cache_probs, cache_values, preferred_element_type=jnp.float32
    )
    mixed_heads = mixed_heads + jnp.einsum(
        "trkgs,srkd->trkgd", new_probs, new_values, preferred_element_type=jnp.float32
    )
    return mixed_heads.reshape(step_count, row_count, row_width).astype(jnp.bfloat16)


def project_kernel(fresh, acts, stream, out, wsend, wbuf, asend, abuf, part, r1, rb, s2, r2, q, u1, ub, v2, u2, fin,
                   loc_sem, send_sem, recv_sem):
    z, y_lo, core, x, y_hi = coords()
    y, mp, slot = y_hi * 2 + y_lo, x * 2 + y_hi, z * 2 + core

    def at_y(yy):
        return place(z, yy % 2, core, x, yy // 2)

    sib = place(z, y_lo, 1 - core, x, y_hi)
    z_up, z_down = place((z + 1) % 4, y_lo, core, x, y_hi), place((z + 3) % 4, y_lo, core, x, y_hi)
    x_up, x_down = place(z, y_lo, core, (x + 1) % 4, y_hi), place(z, y_lo, core, (x + 3) % 4, y_hi)
    y_up, y_down = at_y((y + 1) % 4), at_y((y + 3) % 4)
    across = place(z, 1 - y_lo, core, x, y_hi)
    peers = []
    for i in range(1, 8):
        dx, dy = i // 2, i % 2
        peers.append((((x + dx) % 4), ((y_hi + dy) % 2)))
    peer_place = [place(z, y_lo, core, px, py) for px, py in peers]

    barrier = pltpu.get_barrier_semaphore()
    everyone = peer_place + [sib, z_up, z_down, y_up, y_down]
    for other in everyone:
        pl.semaphore_signal(barrier, inc=1, device_id=other, device_id_type=MESHID)
    pl.semaphore_wait(barrier, len(everyone))

    count = [0]
    sends = []

    def send(src, dst, device):
        i = count[0]
        count[0] += 1
        copy = pltpu.make_async_remote_copy(
            src_ref=src, dst_ref=dst, send_sem=send_sem.at[i], recv_sem=recv_sem.at[i],
            device_id=device, device_id_type=MESHID)
        copy.start()
        sends.append(copy)
        return copy

    st = {}

    row = lax.broadcasted_iota(jnp.int32, (128, 120), 0)
    col = lax.broadcasted_iota(jnp.int32, (128, 120), 1)
    pick = jnp.where(col == (row % 16) * 8 + row // 16, 1.0, 0.0).astype(bf16)
    for b in range(8):
        p = jnp.dot(pick, fresh[:, b * 512:(b + 1) * 512], preferred_element_type=f32).astype(bf16)
        for k in range(4):
            wsend[k, :, :, b * 128:(b + 1) * 128] = p[:, k * 128:(k + 1) * 128].reshape(8, 16, 128)

    def spread(k):
        st["a", k] = []
        st["l", k] = pltpu.make_async_copy(wsend.at[k, mp], wbuf.at[k, mp, slot], loc_sem.at[k])
        st["l", k].start()
        for (px, py), device in zip(peers, peer_place):
            st["a", k].append(send(wsend.at[k, px * 2 + py], wbuf.at[k, mp, slot], device))

    spread(0)

    unit = lax.broadcasted_iota(jnp.int32, (384, 256), 0)
    lane = lax.broadcasted_iota(jnp.int32, (384, 256), 1)
    own = (lane % 128) // 16
    target = ((own // 2) * 4 + (lane // 128) * 2 + own % 2) * 15 + lane % 16
    target = jnp.where(lane % 16 < 15, target, -1000)
    for b in range(8):
        start, shift = (b * 240) // 128 * 128, (b * 240) % 128
        depth = 256 if shift + 240 <= 256 else 384
        e = jnp.where(unit[:depth] - shift == target[:depth], 1.0, 0.0).astype(bf16)
        a = jnp.dot(acts[:, start:start + depth], e, preferred_element_type=f32).astype(bf16)
        asend[0, :, b * 128:(b + 1) * 128] = a[:, :128]
        asend[1, :, b * 128:(b + 1) * 128] = a[:, 128:]
    swap = send(asend.at[1 - y_lo], abuf.at[y_lo], across)
    abuf[y_lo] = asend[y_lo]
    for k in range(1, 4):
        spread(k)

    def gather_start(k):
        st["l", k].wait()
        for copy in st["a", k]:
            copy.wait_recv()
        mine = wbuf.at[k, :, slot]
        st["u", k] = send(mine, wbuf.at[k, :, slot], z_up)
        st["d", k] = send(mine, wbuf.at[k, :, slot], z_down)
        st["s", k] = [send(mine, wbuf.at[k, :, slot], sib)]

    def gather_mid(k):
        below, above = ((z + 3) % 4) * 2 + core, ((z + 1) % 4) * 2 + core
        st["u", k].wait_recv()
        low = wbuf.at[k, pl.ds(0, 4), below]
        st["ru", k] = send(low, wbuf.at[k, pl.ds(0, 4), below], z_up)
        st["d", k].wait_recv()
        high = wbuf.at[k, pl.ds(4, 4), above]
        st["rd", k] = send(high, wbuf.at[k, pl.ds(4, 4), above], z_down)
        st["s", k].append(send(wbuf.at[k, :, below], wbuf.at[k, :, below], sib))
        st["s", k].append(send(wbuf.at[k, :, above], wbuf.at[k, :, above], sib))

    def gather_end(k):
        far = ((z + 2) % 4) * 2 + core
        st["ru", k].wait_recv()
        st["rd", k].wait_recv()
        st["s", k].append(send(wbuf.at[k, :, far], wbuf.at[k, :, far], sib))

    def multiply(k):
        for copy in st["s", k]:
            copy.wait_recv()
        if k == 0:
            swap.wait_recv()
        lhs = abuf[...].reshape(384, 1024)

        def body(n, carry):
            cols = pl.ds(pl.multiple_of(n * 256, 256), 256)
            rhs = wbuf[k, :, :, :, cols].reshape(1024, 256)
            p = jnp.dot(lhs, rhs, preferred_element_type=f32).astype(bf16)
            for i in range(4):
                piece = p[(i % 2) * 192:(i % 2 + 1) * 192, (i // 2) * 128:(i // 2 + 1) * 128]
                if k % 2 == 0:
                    part[k, n, i] = piece
                else:
                    part[k, i, n] = piece
            return carry

        lax.fori_loop(0, 4, body, 0)
        me, up, down = (x, x_up, x_down) if k % 2 == 0 else (y, y_up, y_down)
        far, above, below = (me + 2) % 4, (me + 1) % 4, (me + 3) % 4
        lo, hi = pl.ds(0, 2), pl.ds(2, 2)
        st["r1", k] = [send(part.at[k, far, lo], r1.at[k, 0], up), send(part.at[k, far, hi], r1.at[k, 1], down)]
        st["rb", k] = [send(part.at[k, above, hi], rb.at[k, 0], up), send(part.at[k, below, lo], rb.at[k, 1], down)]

    def first_mid(k):
        me, up, down = (x, x_up, x_down) if k % 2 == 0 else (y, y_up, y_down)
        above, below = (me + 1) % 4, (me + 3) % 4
        st["r1", k][0].wait_recv()
        s2[k, 0] = (part[k, above, pl.ds(0, 2)].astype(f32) + r1[k, 0].astype(f32)).astype(bf16)
        a = send(s2.at[k, 0], r2.at[k, 0], up)
        st["r1", k][1].wait_recv()
        s2[k, 1] = (part[k, below, pl.ds(2, 2)].astype(f32) + r1[k, 1].astype(f32)).astype(bf16)
        st["r2", k] = [a, send(s2.at[k, 1], r2.at[k, 1], down)]

    def first_end(k):
        me = x if k % 2 == 0 else y
        st["rb", k][1].wait_recv()
        st["r2", k][0].wait_recv()
        q[k, pl.ds(0, 2)] = (part[k, me, pl.ds(0, 2)].astype(f32) + rb[k, 1].astype(f32) + r2[k, 0].astype(f32)).astype(bf16)
        st["rb", k][0].wait_recv()
        st["r2", k][1].wait_recv()
        q[k, pl.ds(2, 2)] = (part[k, me, pl.ds(2, 2)].astype(f32) + rb[k, 0].astype(f32) + r2[k, 1].astype(f32)).astype(bf16)
        other, up, down = (y, y_up, y_down) if k % 2 == 0 else (x, x_up, x_down)
        far, above, below = (other + 2) % 4, (other + 1) % 4, (other + 3) % 4
        lo, hi = pl.ds(0, 96), pl.ds(96, 96)
        st["u1", k] = [send(q.at[k, far, lo], u1.at[k, 0], up), send(q.at[k, far, hi], u1.at[k, 1], down)]
        st["ub", k] = [send(q.at[k, above, hi], ub.at[k, 0], up), send(q.at[k, below, lo], ub.at[k, 1], down)]

    def second_mid(k):
        other, up, down = (y, y_up, y_down) if k % 2 == 0 else (x, x_up, x_down)
        above, below = (other + 1) % 4, (other + 3) % 4
        st["u1", k][0].wait_recv()
        v2[k, 0] = (q[k, above, pl.ds(0, 96)].astype(f32) + u1[k, 0].astype(f32)).astype(bf16)
        a = send(v2.at[k, 0], u2.at[k, 0], up)
        st["u1", k][1].wait_recv()
        v2[k, 1] = (q[k, below, pl.ds(96, 96)].astype(f32) + u1[k, 1].astype(f32)).astype(bf16)
        st["u2", k] = [a, send(v2.at[k, 1], u2.at[k, 1], down)]

    def second_end(k):
        other = y if k % 2 == 0 else x
        cols = pl.ds(k * 128, 128)
        st["ub", k][1].wait_recv()
        st["u2", k][0].wait_recv()
        lo = q[k, other, pl.ds(0, 96)].astype(f32) + ub[k, 1].astype(f32) + u2[k, 0].astype(f32)
        out[pl.ds(0, 96), cols] = (stream[pl.ds(0, 96), cols].astype(f32) + lo).astype(bf16)
        st["ub", k][0].wait_recv()
        st["u2", k][1].wait_recv()
        hi = q[k, other, pl.ds(96, 96)].astype(f32) + ub[k, 0].astype(f32) + u2[k, 1].astype(f32)
        out[pl.ds(96, 96), cols] = (stream[pl.ds(96, 96), cols].astype(f32) + hi).astype(bf16)

    A, B, C, D, E, F, G, H = (gather_start, gather_mid, gather_end, multiply, first_mid, first_end, second_mid, second_end)
    A(0); A(1); B(0); A(2); C(0); B(1); D(0); A(3); C(1); B(2); E(0); D(1); C(2); B(3); F(0); E(1); D(2); C(3)
    G(0); F(1); E(2); D(3); H(0); G(1); F(2); E(3); H(1); G(2); F(3); H(2); G(3); H(3)
    for copy in sends:
        copy.wait_send()


def project(fresh, acts, stream):
    copies = 4 * 27 + 1
    return pl.pallas_call(
        project_kernel,
        out_shape=jax.ShapeDtypeStruct((192, 512), bf16),
        in_specs=[pl.BlockSpec(memory_space=pltpu.VMEM)] * 3,
        out_specs=pl.BlockSpec(memory_space=pltpu.VMEM),
        scratch_shapes=[
            pltpu.VMEM((4, 8, 16, 1024), bf16),
            pltpu.VMEM((4, 8, 8, 16, 1024), bf16),
            pltpu.VMEM((2, 192, 1024), bf16),
            pltpu.VMEM((2, 192, 1024), bf16),
            pltpu.VMEM((4, 4, 4, 192, 128), bf16),
            *[pltpu.VMEM((4, 2, 2, 192, 128), bf16)] * 4,
            pltpu.VMEM((4, 4, 192, 128), bf16),
            *[pltpu.VMEM((4, 2, 96, 128), bf16)] * 4,
            pltpu.VMEM((8, 128), f32),
            pltpu.SemaphoreType.DMA((4,)),
            pltpu.SemaphoreType.DMA((copies,)),
            pltpu.SemaphoreType.DMA((copies,)),
        ],
        compiler_params=pltpu.CompilerParams(collective_id=1, has_side_effects=True, vmem_limit_bytes=52 * 2**20),
        cost_estimate=pl.CostEstimate(flops=3221225472, bytes_accessed=4 * 2**20, transcendentals=0),
        name="project",
    )(fresh, acts, stream)


def local(
    learn_hidden,
    out_cot,
    master,
    moment_one,
    moment_two,
    queries,
    keys_cache,
    values_cache,
    keys_new,
    values_new,
    lengths,
    residual,
    unit_acts,
):
    gradient_rows = grad_sum(learn_hidden, out_cot)
    moment_one_next = beta_one * moment_one + (1.0 - beta_one) * gradient_rows
    moment_two_next = beta_two * moment_two + (1.0 - beta_two) * gradient_rows * gradient_rows
    first_hat = moment_one_next / (1.0 - beta_one**bias_steps)
    second_hat = moment_two_next / (1.0 - beta_two**bias_steps)
    master_next = master - learn_rate * (
        first_hat / (jnp.sqrt(second_hat) + adam_eps) + decay_rate * master
    )
    fresh_rows = master_next.astype(jnp.bfloat16)
    attended = attend(queries, keys_cache, values_cache, keys_new, values_new, lengths)
    stream = (residual.astype(jnp.float32) + attended.astype(jnp.float32)).astype(jnp.bfloat16)
    mixed = project(fresh_rows, unit_acts.reshape(192, 1920), stream.reshape(192, 512)).reshape(stream.shape)
    return (mixed, master_next, moment_one_next, moment_two_next)


def solution(mesh):
    placed = (
        P("dp", "mp"),
        P("dp", None),
        P(("mp", "dp"), None),
        P(("mp", "dp"), None),
        P(("mp", "dp"), None),
        P(None, "dp", "mp"),
        P("dp", None, "mp"),
        P("dp", None, "mp"),
        P(None, "dp", "mp"),
        P(None, "dp", "mp"),
        P("dp"),
        P(None, "dp", "mp"),
        P(None, "dp", "mp", None),
    )
    return jax.shard_map(
        local,
        mesh=mesh,
        in_specs=placed,
        out_specs=(
            P(None, "dp", "mp"),
            P(("mp", "dp"), None),
            P(("mp", "dp"), None),
            P(("mp", "dp"), None),
        ),
        check_vma=False,
    )
```

```python
import functools
import jax
import jax.numpy as jnp
from jax import lax
from jax.experimental import pallas as pl
from jax.experimental.pallas import tpu as pltpu
from jax.sharding import PartitionSpec as P

MESHID = pl.DeviceIdType.MESH
bf16, f32 = jnp.bfloat16, jnp.float32
HEADS = 32
KV_HEADS = 8
HEAD_DIM = 128
CHUNKS = 4
KIND = (("Z", "Y"), ("Z", "Y"), ("Z", "Y"), ("Z", "Y"))
ORDER = [
    ("yc", 1, 1), ("zc", 0, 0), ("zm", 0, 0), ("zc", 2, 0), ("yc", 0, 1), ("ze", 0, 0), ("zc", 1, 0), ("ys", 1, 1),
    ("zm", 2, 0), ("zm", 1, 0), ("ym", 1, 1), ("yc", 2, 1), ("ys", 0, 1), ("zf", 0, 0), ("ym", 0, 1), ("ye", 1, 1),
    ("zc", 3, 0), ("ye", 0, 1), ("ze", 1, 0), ("ad", 0), ("zm", 3, 0), ("ys", 2, 1), ("ze", 2, 0), ("zf", 1, 0),
    ("ym", 2, 1), ("ad", 1), ("ga", 0), ("yc", 3, 1), ("ga", 1), ("ze", 3, 0), ("ye", 2, 1), ("zf", 2, 0), ("gb", 0),
    ("ad", 2), ("gb", 1), ("gc", 0), ("ys", 3, 1), ("mm", 0), ("ym", 3, 1), ("zf", 3, 0), ("gc", 1), ("ga", 2),
    ("ye", 3, 1), ("f2", 0), ("ad", 3), ("gb", 2), ("mm", 1), ("ga", 3), ("f3", 0), ("gc", 2), ("mm", 2), ("gb", 3),
    ("f2", 2), ("gc", 3), ("f4", 0), ("f2", 1), ("mm", 3), ("f3", 1), ("f2", 3), ("f3", 2), ("f4", 1), ("f3", 3),
    ("f4", 2), ("f5", 0), ("f4", 3), ("f5", 1), ("f5", 2), ("f5", 3),
]
beta_one = 0.9
beta_two = 0.999
learn_rate = 0.01
decay_rate = 0.1
adam_eps = 1e-08
bias_steps = 10.0


def coords():
    dp, mp = lax.axis_index("dp"), lax.axis_index("mp")
    return dp // 4, (dp // 2) % 2, dp % 2, mp // 2, mp % 2


def place(z, y_lo, core, x, y_hi):
    return ((z * 2 + y_lo) * 2 + core, x * 2 + y_hi)


def fused_kernel(ht, cot, acts, stream, master, first, second, out, grad,
                 hs, cs, zs1, zsb, zs2, zr1, zrb, zr2, zhold, zown, zys, zyr,
                 yys, yyr, ys1, ysb, ys2, yr1, yrb, yr2, yhold, yown, gbuf, gall, adam,
                 wsend, wbuf, asend, abuf, part, r1, rb, s2, r2, q, u1, ub, v2, u2,
                 loc_sem, send_sem, recv_sem):
    z, y_lo, core, x, y_hi = coords()
    y, mp, slot = y_hi * 2 + y_lo, x * 2 + y_hi, z * 2 + core

    def at_y(yy):
        return place(z, yy % 2, core, x, yy // 2)

    sib = place(z, y_lo, 1 - core, x, y_hi)
    z_up, z_down = place((z + 1) % 4, y_lo, core, x, y_hi), place((z + 3) % 4, y_lo, core, x, y_hi)
    x_up, x_down = place(z, y_lo, core, (x + 1) % 4, y_hi), place(z, y_lo, core, (x + 3) % 4, y_hi)
    y_up, y_down = at_y((y + 1) % 4), at_y((y + 3) % 4)
    across = place(z, 1 - y_lo, core, x, y_hi)
    peers = [((x + i // 2) % 4, (y_hi + i % 2) % 2) for i in range(1, 8)]
    peer_place = [place(z, y_lo, core, px, py) for px, py in peers]

    barrier = pltpu.get_barrier_semaphore()
    everyone = peer_place + [sib, z_up, z_down, y_up, y_down]
    for other in everyone:
        pl.semaphore_signal(barrier, inc=1, device_id=other, device_id_type=MESHID)
    pl.semaphore_wait(barrier, len(everyone))

    count = [0, 0]
    sends = []
    st = {}

    def send(src, dst, device):
        i = count[0]
        count[0] += 1
        copy = pltpu.make_async_remote_copy(
            src_ref=src, dst_ref=dst, send_sem=send_sem.at[i], recv_sem=recv_sem.at[i],
            device_id=device, device_id_type=MESHID)
        copy.start()
        sends.append(copy)
        return copy

    def local(src, dst):
        i = count[1]
        count[1] += 1
        copy = pltpu.make_async_copy(src, dst, loc_sem.at[i])
        copy.start()
        return copy

    h_own = local(ht, hs.at[:, :, pl.ds(0, 512)])
    h_sib = send(ht, hs.at[:, :, pl.ds(512, 512)], sib)
    for k in range(4):
        for h in range(2):
            st["c", k, h] = []
            for i in range(2):
                mine = pl.ds(pl.multiple_of((4 * core + 2 * h + i) * 512 + k * 128, 128), 128)
                theirs = pl.ds(pl.multiple_of((4 - 4 * core + 2 * h + i) * 512 + k * 128, 128), 128)
                lanes = pl.ds(i * 128, 128)
                st["c", k, h].append(send(cot.at[:, theirs], cs.at[k, h, pl.ds(512, 512), lanes], sib))
                st["c", k, h].append(local(cot.at[:, mine], cs.at[k, h, pl.ds(0, 512), lanes]))

    def adam_fetch(k):
        for b in range(8):
            for i, ref in enumerate((master, first, second)):
                st["m", k, b, i] = local(ref.at[:, pl.ds(b * 512 + k * 128, 128)], adam.at[k % 2, i, b])

    adam_fetch(0)

    unit = lax.broadcasted_iota(jnp.int32, (384, 256), 0)
    lane = lax.broadcasted_iota(jnp.int32, (384, 256), 1)
    owner = (lane % 128) // 16
    target = ((owner // 2) * 4 + (lane // 128) * 2 + owner % 2) * 15 + lane % 16
    target = jnp.where(lane % 16 < 15, target, -1000)
    for b in range(8):
        start, shift = (b * 240) // 128 * 128, (b * 240) % 128
        depth = 256 if shift + 240 <= 256 else 384
        e = jnp.where(unit[:depth] - shift == target[:depth], 1.0, 0.0).astype(bf16)
        a = jnp.dot(acts[:, start:start + depth], e, preferred_element_type=f32).astype(bf16)
        asend[0, :, b * 128:(b + 1) * 128] = a[:, :128]
        asend[1, :, b * 128:(b + 1) * 128] = a[:, 128:]
    swap = send(asend.at[1 - y_lo], abuf.at[y_lo], across)
    abuf[y_lo] = asend[y_lo]

    h_own.wait()
    h_sib.wait_recv()

    def ready(k, h):
        for i in range(2):
            st["c", k, h][2 * i].wait_recv()
            st["c", k, h][2 * i + 1].wait()

    zp, zm, zf = (z + 1) % 4, (z + 3) % 4, (z + 2) % 4

    def ring_start(key, term, s1, sb, r1, rb, hold, own):
        p = term(zf)
        s1[0] = p[:, :128].astype(bf16)
        s1[1] = p[:, 128:].astype(bf16)
        st["r1", key] = [send(s1.at[0], r1.at[0], z_up), send(s1.at[1], r1.at[1], z_down)]
        p = term(zp)
        sb[0] = p[:, 128:].astype(bf16)
        b0 = send(sb.at[0], rb.at[0], z_up)
        hold[0] = p[:, :128].astype(hold.dtype)
        p = term(zm)
        sb[1] = p[:, :128].astype(bf16)
        b1 = send(sb.at[1], rb.at[1], z_down)
        hold[1] = p[:, 128:].astype(hold.dtype)
        st["rb", key] = [b0, b1]
        own[...] = term(z)

    def ring_mid(key, s2, r1, r2, hold):
        st["r2", key] = []
        for d, device in ((0, z_up), (1, z_down)):
            st["r1", key][d].wait_recv()
            s2[d] = (hold[d].astype(f32) + r1[d].astype(f32)).astype(bf16)
            st["r2", key].append(send(s2.at[d], r2.at[d], device))

    def ring_end(key, rb, r2, own):
        st["rb", key][1].wait_recv()
        st["r2", key][0].wait_recv()
        left = own[:, :128] + rb[1].astype(f32) + r2[0].astype(f32)
        st["rb", key][0].wait_recv()
        st["r2", key][1].wait_recv()
        right = own[:, 128:] + rb[0].astype(f32) + r2[1].astype(f32)
        return left, right

    def finish(k, h, left, right):
        gbuf[k, h, :, :, pl.ds(0, 128)] = left.reshape(2, 120, 128)
        gbuf[k, h, :, :, pl.ds(128, 128)] = right.reshape(2, 120, 128)
        st["g", k, h] = send(gbuf.at[k, h, 1 - core], gall.at[k, core, h], sib)
        gall[k, core, h] = gbuf[k, h, core]

    numbers = {"Z": 0, "Y": 0}
    index = {}
    for k in range(4):
        for h in range(2):
            index[k, h] = numbers[KIND[k][h]]
            numbers[KIND[k][h]] += 1

    def zc(k, h):
        n = index[k, h]
        ready(k, h)

        def term(zb):
            return jnp.dot(hs[pl.ds(2 * zb, 2)].reshape(480, 1024), cs[k, h], preferred_element_type=f32)

        ring_start(("z", n), term, zs1.at[n], zsb.at[n], zr1.at[n], zrb.at[n], zhold.at[n], zown.at[n])

    def zm_(k, h):
        n = index[k, h]
        ring_mid(("z", n), zs2.at[n], zr1.at[n], zr2.at[n], zhold.at[n])

    def ze(k, h):
        n = index[k, h]
        left, right = ring_end(("z", n), zrb.at[n], zr2.at[n], zown.at[n])
        zown[n, :, pl.ds(0, 128)] = left
        zown[n, :, pl.ds(128, 128)] = right
        theirs = pl.ds(pl.multiple_of((1 - y_lo) * 240, 16), 240)
        zys[n] = zown[n, theirs, :].astype(bf16)
        st["zy", n] = send(zys.at[n], zyr.at[n], across)

    def zf_(k, h):
        n = index[k, h]
        st["zy", n].wait_recv()
        mine = pl.ds(pl.multiple_of(y_lo * 240, 16), 240)
        total = zown[n, mine, :] + zyr[n].astype(f32)
        finish(k, h, total[:, :128], total[:, 128:])

    def yc(k, h):
        n = index[k, h]
        ready(k, h)

        def body(zb, carry):
            yys[n, zb] = jnp.dot(hs[2 * zb + 1 - y_lo], cs[k, h], preferred_element_type=f32).astype(bf16)
            return carry

        lax.fori_loop(0, 4, body, 0)
        st["yy", n] = send(yys.at[n], yyr.at[n], across)

    def ys(k, h):
        n = index[k, h]
        st["yy", n].wait_recv()

        def term(zb):
            return jnp.dot(hs[2 * zb + y_lo], cs[k, h], preferred_element_type=f32) + yyr[n, zb].astype(f32)

        ring_start(("y", n), term, ys1.at[n], ysb.at[n], yr1.at[n], yrb.at[n], yhold.at[n], yown.at[n])

    def ym(k, h):
        n = index[k, h]
        ring_mid(("y", n), ys2.at[n], yr1.at[n], yr2.at[n], yhold.at[n])

    def ye(k, h):
        n = index[k, h]
        left, right = ring_end(("y", n), yrb.at[n], yr2.at[n], yown.at[n])
        finish(k, h, left, right)

    def ad(k):
        for h in range(2):
            st["g", k, h].wait_recv()
        if k < 3:
            adam_fetch(k + 1)
        row = lax.broadcasted_iota(jnp.int32, (128, 120), 0)
        col = lax.broadcasted_iota(jnp.int32, (128, 120), 1)
        pick = jnp.where(col == (row % 16) * 8 + row // 16, 1.0, 0.0).astype(bf16)
        for b in range(8):
            for i in range(3):
                st["m", k, b, i].wait()
            g = gall[k, b // 4, (b // 2) % 2, :, (b % 2) * 128:(b % 2 + 1) * 128]
            st["o", k, b] = local(gall.at[k, b // 4, (b // 2) % 2, :, pl.ds((b % 2) * 128, 128)],
                                  grad.at[:, pl.ds(b * 512 + k * 128, 128)])
            m = adam[k % 2, 0, b]
            one = beta_one * adam[k % 2, 1, b] + (1.0 - beta_one) * g
            two = beta_two * adam[k % 2, 2, b] + (1.0 - beta_two) * g * g
            one_hat = one / (1.0 - beta_one**bias_steps)
            two_hat = two / (1.0 - beta_two**bias_steps)
            new = m - learn_rate * (one_hat / (jnp.sqrt(two_hat) + adam_eps) + decay_rate * m)
            p = jnp.dot(pick, new.astype(bf16), preferred_element_type=f32).astype(bf16)
            wsend[k, :, :, b * 128:(b + 1) * 128] = p.reshape(8, 16, 128)
        st["l", k] = local(wsend.at[k, mp], wbuf.at[k, mp, slot])
        st["a", k] = []
        for (px, py), device in zip(peers, peer_place):
            st["a", k].append(send(wsend.at[k, px * 2 + py], wbuf.at[k, mp, slot], device))

    def ga(k):
        st["l", k].wait()
        for copy in st["a", k]:
            copy.wait_recv()
        mine = wbuf.at[k, :, slot]
        st["u", k] = send(mine, mine, z_up)
        st["d", k] = send(mine, mine, z_down)
        st["s", k] = [send(mine, mine, sib)]

    def gb(k):
        below, above = ((z + 3) % 4) * 2 + core, ((z + 1) % 4) * 2 + core
        st["u", k].wait_recv()
        low = wbuf.at[k, pl.ds(0, 4), below]
        st["ru", k] = send(low, low, z_up)
        st["d", k].wait_recv()
        high = wbuf.at[k, pl.ds(4, 4), above]
        st["rd", k] = send(high, high, z_down)
        for s in (below, above):
            st["s", k].append(send(wbuf.at[k, :, s], wbuf.at[k, :, s], sib))

    def gc(k):
        far = ((z + 2) % 4) * 2 + core
        st["ru", k].wait_recv()
        st["rd", k].wait_recv()
        st["s", k].append(send(wbuf.at[k, :, far], wbuf.at[k, :, far], sib))

    def mm(k):
        for copy in st["s", k]:
            copy.wait_recv()
        if "swap" not in st:
            swap.wait_recv()
            st["swap"] = True
        lhs = abuf[...].reshape(384, 1024)

        def body(n, carry):
            cols = pl.ds(pl.multiple_of(n * 256, 256), 256)
            rhs = wbuf[k, :, :, :, cols].reshape(1024, 256)
            p = jnp.dot(lhs, rhs, preferred_element_type=f32).astype(bf16)
            for i in range(4):
                part[k, n, i] = p[(i % 2) * 192:(i % 2 + 1) * 192, (i // 2) * 128:(i // 2 + 1) * 128]
            return carry

        lax.fori_loop(0, 4, body, 0)
        far, above, below = (x + 2) % 4, (x + 1) % 4, (x + 3) % 4
        lo, hi = pl.ds(0, 2), pl.ds(2, 2)
        st["f1", k] = [send(part.at[k, far, lo], r1.at[k, 0], x_up), send(part.at[k, far, hi], r1.at[k, 1], x_down)]
        st["fb", k] = [send(part.at[k, above, hi], rb.at[k, 0], x_up), send(part.at[k, below, lo], rb.at[k, 1], x_down)]

    def f2(k):
        above, below = (x + 1) % 4, (x + 3) % 4
        st["f1", k][0].wait_recv()
        s2[k, 0] = (part[k, above, pl.ds(0, 2)].astype(f32) + r1[k, 0].astype(f32)).astype(bf16)
        a = send(s2.at[k, 0], r2.at[k, 0], x_up)
        st["f1", k][1].wait_recv()
        s2[k, 1] = (part[k, below, pl.ds(2, 2)].astype(f32) + r1[k, 1].astype(f32)).astype(bf16)
        st["f2", k] = [a, send(s2.at[k, 1], r2.at[k, 1], x_down)]

    def f3(k):
        st["fb", k][1].wait_recv()
        st["f2", k][0].wait_recv()
        q[k, pl.ds(0, 2)] = (part[k, x, pl.ds(0, 2)].astype(f32) + rb[k, 1].astype(f32) + r2[k, 0].astype(f32)).astype(bf16)
        st["fb", k][0].wait_recv()
        st["f2", k][1].wait_recv()
        q[k, pl.ds(2, 2)] = (part[k, x, pl.ds(2, 2)].astype(f32) + rb[k, 0].astype(f32) + r2[k, 1].astype(f32)).astype(bf16)
        far, above, below = (y + 2) % 4, (y + 1) % 4, (y + 3) % 4
        lo, hi = pl.ds(0, 96), pl.ds(96, 96)
        st["g1", k] = [send(q.at[k, far, lo], u1.at[k, 0], y_up), send(q.at[k, far, hi], u1.at[k, 1], y_down)]
        st["gb", k] = [send(q.at[k, above, hi], ub.at[k, 0], y_up), send(q.at[k, below, lo], ub.at[k, 1], y_down)]

    def f4(k):
        above, below = (y + 1) % 4, (y + 3) % 4
        st["g1", k][0].wait_recv()
        v2[k, 0] = (q[k, above, pl.ds(0, 96)].astype(f32) + u1[k, 0].astype(f32)).astype(bf16)
        a = send(v2.at[k, 0], u2.at[k, 0], y_up)
        st["g1", k][1].wait_recv()
        v2[k, 1] = (q[k, below, pl.ds(96, 96)].astype(f32) + u1[k, 1].astype(f32)).astype(bf16)
        st["g2", k] = [a, send(v2.at[k, 1], u2.at[k, 1], y_down)]

    def f5(k):
        cols = pl.ds(k * 128, 128)
        st["gb", k][1].wait_recv()
        st["g2", k][0].wait_recv()
        lo = q[k, y, pl.ds(0, 96)].astype(f32) + ub[k, 1].astype(f32) + u2[k, 0].astype(f32)
        out[pl.ds(0, 96), cols] = (stream[pl.ds(0, 96), cols].astype(f32) + lo).astype(bf16)
        st["gb", k][0].wait_recv()
        st["g2", k][1].wait_recv()
        hi = q[k, y, pl.ds(96, 96)].astype(f32) + ub[k, 0].astype(f32) + u2[k, 1].astype(f32)
        out[pl.ds(96, 96), cols] = (stream[pl.ds(96, 96), cols].astype(f32) + hi).astype(bf16)

    steps = {"zc": zc, "zm": zm_, "ze": ze, "zf": zf_, "yc": yc, "ys": ys, "ym": ym, "ye": ye, "ad": ad,
             "ga": ga, "gb": gb, "gc": gc, "mm": mm, "f2": f2, "f3": f3, "f4": f4, "f5": f5}
    for name, *where in ORDER:
        steps[name](*where)
    for k in range(4):
        for b in range(8):
            st["o", k, b].wait()
    for copy in sends:
        copy.wait_send()


def fused(learn_hidden, out_cot, acts, stream, master, first, second):
    ht = learn_hidden.T.reshape(8, 240, 512)
    kinds = [a for pair in KIND for a in pair]
    nz, ny = max(kinds.count("Z"), 1), max(kinds.count("Y"), 1)

    def ring(n, r):
        return [pltpu.VMEM((n, 2, r, 128), bf16)] * 7 + [pltpu.VMEM((n, r, 256), f32)]

    copies = 1 + 16 + 1 + 8 * 8 + 4 * 27
    locals_ = 1 + 16 + 4 * (24 + 8 + 1)
    return pl.pallas_call(
        fused_kernel,
        out_shape=(jax.ShapeDtypeStruct((192, 512), bf16), jax.ShapeDtypeStruct((120, 4096), f32)),
        in_specs=[pl.BlockSpec(memory_space=pl.ANY)] * 2 + [pl.BlockSpec(memory_space=pltpu.VMEM)] * 2
        + [pl.BlockSpec(memory_space=pl.ANY)] * 3,
        out_specs=(pl.BlockSpec(memory_space=pltpu.VMEM), pl.BlockSpec(memory_space=pl.ANY)),
        scratch_shapes=[
            pltpu.VMEM((8, 240, 1024), bf16),
            pltpu.VMEM((4, 2, 1024, 256), bf16),
            *ring(nz, 480),
            pltpu.VMEM((nz, 240, 256), bf16),
            pltpu.VMEM((nz, 240, 256), bf16),
            pltpu.VMEM((ny, 4, 240, 256), bf16),
            pltpu.VMEM((ny, 4, 240, 256), bf16),
            *ring(ny, 240),
            pltpu.VMEM((4, 2, 2, 120, 256), f32),
            pltpu.VMEM((4, 2, 2, 120, 256), f32),
            pltpu.VMEM((2, 3, 8, 120, 128), f32),
            pltpu.VMEM((4, 8, 16, 1024), bf16),
            pltpu.VMEM((4, 8, 8, 16, 1024), bf16),
            pltpu.VMEM((2, 192, 1024), bf16),
            pltpu.VMEM((2, 192, 1024), bf16),
            pltpu.VMEM((4, 4, 4, 192, 128), bf16),
            *[pltpu.VMEM((4, 2, 2, 192, 128), bf16)] * 4,
            pltpu.VMEM((4, 4, 192, 128), bf16),
            *[pltpu.VMEM((4, 2, 96, 128), bf16)] * 4,
            pltpu.SemaphoreType.DMA((locals_,)),
            pltpu.SemaphoreType.DMA((copies,)),
            pltpu.SemaphoreType.DMA((copies,)),
        ],
        compiler_params=pltpu.CompilerParams(collective_id=0, has_side_effects=True, vmem_limit_bytes=60 * 2**20),
        cost_estimate=pl.CostEstimate(flops=11274289152, bytes_accessed=20 * 2**20, transcendentals=0),
        name="fused",
    )(ht, out_cot, acts, stream, master, first, second)


def attend(queries, keys_cache, values_cache, keys_new, values_new, lengths):
    step_count, row_count, row_width = queries.shape
    cache_len = keys_cache.shape[1]
    kv_local = keys_cache.shape[2] // HEAD_DIM
    per_group = HEADS // KV_HEADS
    query_heads = queries.reshape(step_count, row_count, kv_local, per_group, HEAD_DIM)
    cache_keys = keys_cache.reshape(row_count, cache_len, kv_local, HEAD_DIM)
    cache_values = values_cache.reshape(row_count, cache_len, kv_local, HEAD_DIM)
    new_keys = keys_new.reshape(step_count, row_count, kv_local, HEAD_DIM)
    new_values = values_new.reshape(step_count, row_count, kv_local, HEAD_DIM)
    score_scale = HEAD_DIM ** (-0.5)
    cache_scores = (
        jnp.einsum("trkgd,rlkd->trkgl", query_heads, cache_keys, preferred_element_type=jnp.float32)
        * score_scale
    )
    new_scores = (
        jnp.einsum("trkgd,srkd->trkgs", query_heads, new_keys, preferred_element_type=jnp.float32)
        * score_scale
    )
    visible = jnp.arange(cache_len)[None, :] < lengths[:, None]
    causal = jnp.arange(step_count)[:, None] >= jnp.arange(step_count)[None, :]
    cache_scores = jnp.where(visible[None, :, None, None, :], cache_scores, -jnp.inf)
    new_scores = jnp.where(causal[:, None, None, None, :], new_scores, -jnp.inf)
    highest = jnp.maximum(jnp.max(cache_scores, axis=-1), jnp.max(new_scores, axis=-1))
    cache_exp = jnp.exp(cache_scores - highest[..., None])
    new_exp = jnp.exp(new_scores - highest[..., None])
    exp_total = jnp.sum(cache_exp, axis=-1) + jnp.sum(new_exp, axis=-1)
    cache_probs = (cache_exp / exp_total[..., None]).astype(jnp.bfloat16)
    new_probs = (new_exp / exp_total[..., None]).astype(jnp.bfloat16)
    mixed_heads = jnp.einsum(
        "trkgl,rlkd->trkgd", cache_probs, cache_values, preferred_element_type=jnp.float32
    )
    mixed_heads = mixed_heads + jnp.einsum(
        "trkgs,srkd->trkgd", new_probs, new_values, preferred_element_type=jnp.float32
    )
    return mixed_heads.reshape(step_count, row_count, row_width).astype(jnp.bfloat16)


def local(
    learn_hidden,
    out_cot,
    master,
    moment_one,
    moment_two,
    queries,
    keys_cache,
    values_cache,
    keys_new,
    values_new,
    lengths,
    residual,
    unit_acts,
):
    attended = attend(queries, keys_cache, values_cache, keys_new, values_new, lengths)
    stream = (residual.astype(jnp.float32) + attended.astype(jnp.float32)).astype(jnp.bfloat16)
    mixed, gradient_rows = fused(
        learn_hidden, out_cot, unit_acts.reshape(192, 1920), stream.reshape(192, 512), master, moment_one, moment_two
    )
    mixed = mixed.reshape(stream.shape)
    moment_one_next = beta_one * moment_one + (1.0 - beta_one) * gradient_rows
    moment_two_next = beta_two * moment_two + (1.0 - beta_two) * gradient_rows * gradient_rows
    first_hat = moment_one_next / (1.0 - beta_one**bias_steps)
    second_hat = moment_two_next / (1.0 - beta_two**bias_steps)
    master_next = master - learn_rate * (
        first_hat / (jnp.sqrt(second_hat) + adam_eps) + decay_rate * master
    )
    return (mixed, master_next, moment_one_next, moment_two_next)


def solution(mesh):
    placed = (
        P("dp", "mp"),
        P("dp", None),
        P(("mp", "dp"), None),
        P(("mp", "dp"), None),
        P(("mp", "dp"), None),
        P(None, "dp", "mp"),
        P("dp", None, "mp"),
        P("dp", None, "mp"),
        P(None, "dp", "mp"),
        P(None, "dp", "mp"),
        P("dp"),
        P(None, "dp", "mp"),
        P(None, "dp", "mp", None),
    )
    return jax.shard_map(
        local,
        mesh=mesh,
        in_specs=placed,
        out_specs=(
            P(None, "dp", "mp"),
            P(("mp", "dp"), None),
            P(("mp", "dp"), None),
            P(("mp", "dp"), None),
        ),
        check_vma=False,
    )
```

```python
import functools
import jax
import jax.numpy as jnp
from jax import lax
from jax.experimental import pallas as pl
from jax.experimental.pallas import tpu as pltpu
from jax.sharding import PartitionSpec as P

MESHID = pl.DeviceIdType.MESH
bf16, f32 = jnp.bfloat16, jnp.float32
HEADS = 32
KV_HEADS = 8
HEAD_DIM = 128
CHUNKS = 4
KIND = (("Z", "Y"), ("Z", "Y"), ("Z", "Y"), ("Z", "Y"))
ORDER = [
    ("zc", 1, 0), ("yc", 1, 1), ("zc", 3, 0), ("yc", 0, 1), ("zm", 1, 0), ("zc", 0, 0), ("zm", 0, 0), ("zc", 2, 0),
    ("ap",), ("ze", 0, 0), ("zm", 2, 0), ("yc", 2, 1), ("ys", 0, 1), ("ym", 0, 1), ("ys", 1, 1), ("at", 0),
    ("ze", 1, 0), ("ye", 0, 1), ("zf", 0, 0), ("ym", 1, 1), ("zm", 3, 0), ("ye", 1, 1), ("ad", 0), ("ys", 2, 1),
    ("at", 1), ("zf", 1, 0), ("ze", 2, 0), ("ym", 2, 1), ("ad", 1), ("ga", 0), ("ye", 2, 1), ("yc", 3, 1), ("at", 2),
    ("zf", 2, 0), ("ze", 3, 0), ("ga", 1), ("ad", 2), ("gb", 0), ("gb", 1), ("gc", 0), ("ys", 3, 1), ("mm", 0),
    ("ym", 3, 1), ("gc", 1), ("zf", 3, 0), ("ga", 2), ("ye", 3, 1), ("ad", 3), ("mm", 1), ("gb", 2), ("ga", 3),
    ("at", 3), ("gc", 2), ("f2", 0), ("mm", 2), ("gb", 3), ("at", 4), ("f3", 0), ("f2", 2), ("gc", 3), ("f2", 1),
    ("at", 5), ("mm", 3), ("f2", 3), ("f3", 1), ("f3", 2), ("f3", 3), ("f5", 2), ("f5", 0), ("f5", 1), ("f5", 3),
]
beta_one = 0.9
beta_two = 0.999
learn_rate = 0.01
decay_rate = 0.1
adam_eps = 1e-08
bias_steps = 10.0


def coords():
    dp, mp = lax.axis_index("dp"), lax.axis_index("mp")
    return dp // 4, (dp // 2) % 2, dp % 2, mp // 2, mp % 2


def place(z, y_lo, core, x, y_hi):
    return ((z * 2 + y_lo) * 2 + core, x * 2 + y_hi)


def fused_kernel(ht, cot, acts, queries, keys, values, keys_new, values_new, lengths, residual,
                 master, first, second, out, grad,
                 hs, cs, zs1, zsb, zs2, zr1, zrb, zr2, zhold, zown, zys, zyr,
                 yys, yyr, ys1, ysb, ys2, yr1, yrb, yr2, yhold, yown, gbuf, gall, adam,
                 wsend, wbuf, asend, abuf, part, r1, rb, s2, r2, q, ug, kbuf, vbuf, qbuf, nbuf, att,
                 loc_sem, send_sem, recv_sem):
    z, y_lo, core, x, y_hi = coords()
    y, mp, slot = y_hi * 2 + y_lo, x * 2 + y_hi, z * 2 + core

    def at_y(yy):
        return place(z, yy % 2, core, x, yy // 2)

    sib = place(z, y_lo, 1 - core, x, y_hi)
    z_up, z_down = place((z + 1) % 4, y_lo, core, x, y_hi), place((z + 3) % 4, y_lo, core, x, y_hi)
    x_up, x_down = place(z, y_lo, core, (x + 1) % 4, y_hi), place(z, y_lo, core, (x + 3) % 4, y_hi)
    y_place = [at_y((y + d) % 4) for d in range(1, 4)]
    across = place(z, 1 - y_lo, core, x, y_hi)
    peers = [((x + i // 2) % 4, (y_hi + i % 2) % 2) for i in range(1, 8)]
    peer_place = [place(z, y_lo, core, px, py) for px, py in peers]

    barrier = pltpu.get_barrier_semaphore()
    everyone = peer_place + [sib, z_up, z_down, y_place[0], y_place[2]]
    for other in everyone:
        pl.semaphore_signal(barrier, inc=1, device_id=other, device_id_type=MESHID)
    pl.semaphore_wait(barrier, len(everyone))

    count = [0, 0]
    sends = []
    st = {}

    def send(src, dst, device):
        i = count[0]
        count[0] += 1
        copy = pltpu.make_async_remote_copy(
            src_ref=src, dst_ref=dst, send_sem=send_sem.at[i], recv_sem=recv_sem.at[i],
            device_id=device, device_id_type=MESHID)
        copy.start()
        sends.append(copy)
        return copy

    def local(src, dst):
        i = count[1]
        count[1] += 1
        copy = pltpu.make_async_copy(src, dst, loc_sem.at[i])
        copy.start()
        return copy

    zp, zm, zf = (z + 1) % 4, (z + 3) % 4, (z + 2) % 4
    offset = [2, 1, 3, 0]

    def share_hidden(i):
        blocks = pl.ds(((z + offset[i]) % 4) * 2, 2)
        st["h", i] = [send(ht.at[blocks], hs.at[blocks, :, pl.ds(512, 512)], sib),
                      local(ht.at[blocks], hs.at[blocks, :, pl.ds(0, 512)])]

    def share_cotangent(k, h):
        st["c", k, h] = []
        for i in range(2):
            mine = pl.ds(pl.multiple_of((4 * core + 2 * h + i) * 512 + k * 128, 128), 128)
            theirs = pl.ds(pl.multiple_of((4 - 4 * core + 2 * h + i) * 512 + k * 128, 128), 128)
            lanes = pl.ds(i * 128, 128)
            st["c", k, h].append(send(cot.at[:, theirs], cs.at[k, h, pl.ds(512, 512), lanes], sib))
            st["c", k, h].append(local(cot.at[:, mine], cs.at[k, h, pl.ds(0, 512), lanes]))

    first_use = [where for name, *where in ORDER if name in ("yc", "zc")]
    share_hidden(0)
    share_cotangent(*first_use[0])
    for i in range(1, 4):
        share_hidden(i)
    for where in first_use[1:]:
        share_cotangent(*where)
    st["kv"] = [local(keys, kbuf), local(values, vbuf)]

    def hidden(i):
        if ("got", i) not in st:
            st["got", i] = True
            st["h", i][0].wait_recv()
            st["h", i][1].wait()

    def adam_fetch(k):
        for b in range(8):
            for i, ref in enumerate((master, first, second)):
                st["m", k, b, i] = local(ref.at[:, pl.ds(b * 512 + k * 128, 128)], adam.at[k % 2, i, b])

    adam_fetch(0)

    unit = lax.broadcasted_iota(jnp.int32, (384, 256), 0)
    lane = lax.broadcasted_iota(jnp.int32, (384, 256), 1)
    owner = (lane % 128) // 16
    target = ((owner // 2) * 4 + (lane // 128) * 2 + owner % 2) * 15 + lane % 16
    target = jnp.where(lane % 16 < 15, target, -1000)
    for b in range(8):
        start, shift = (b * 240) // 128 * 128, (b * 240) % 128
        depth = 256 if shift + 240 <= 256 else 384
        e = jnp.where(unit[:depth] - shift == target[:depth], 1.0, 0.0).astype(bf16)
        a = jnp.dot(acts[:, start:start + depth], e, preferred_element_type=f32).astype(bf16)
        asend[0, :, b * 128:(b + 1) * 128] = a[:, :128]
        asend[1, :, b * 128:(b + 1) * 128] = a[:, 128:]
    swap = send(asend.at[1 - y_lo], abuf.at[y_lo], across)
    abuf[y_lo] = asend[y_lo]

    def ready(k, h):
        for i in range(2):
            st["c", k, h][2 * i].wait_recv()
            st["c", k, h][2 * i + 1].wait()

    def ring_start(key, term, s1, sb, r1, rb, hold, own):
        hidden(0)
        p = term(zf)
        s1[0] = p[:, :128].astype(bf16)
        s1[1] = p[:, 128:].astype(bf16)
        st["r1", key] = [send(s1.at[0], r1.at[0], z_up), send(s1.at[1], r1.at[1], z_down)]
        hidden(1)
        p = term(zp)
        sb[0] = p[:, 128:].astype(bf16)
        b0 = send(sb.at[0], rb.at[0], z_up)
        hold[0] = p[:, :128].astype(hold.dtype)
        hidden(2)
        p = term(zm)
        sb[1] = p[:, :128].astype(bf16)
        b1 = send(sb.at[1], rb.at[1], z_down)
        hold[1] = p[:, 128:].astype(hold.dtype)
        st["rb", key] = [b0, b1]
        hidden(3)
        own[...] = term(z)

    def ring_mid(key, s2, r1, r2, hold):
        st["r2", key] = []
        for d, device in ((0, z_up), (1, z_down)):
            st["r1", key][d].wait_recv()
            s2[d] = (hold[d].astype(f32) + r1[d].astype(f32)).astype(bf16)
            st["r2", key].append(send(s2.at[d], r2.at[d], device))

    def ring_end(key, rb, r2, own):
        st["rb", key][1].wait_recv()
        st["r2", key][0].wait_recv()
        left = own[:, :128] + rb[1].astype(f32) + r2[0].astype(f32)
        st["rb", key][0].wait_recv()
        st["r2", key][1].wait_recv()
        right = own[:, 128:] + rb[0].astype(f32) + r2[1].astype(f32)
        return left, right

    def finish(k, h, left, right):
        gbuf[k, h, :, :, pl.ds(0, 128)] = left.reshape(2, 120, 128)
        gbuf[k, h, :, :, pl.ds(128, 128)] = right.reshape(2, 120, 128)
        st["g", k, h] = send(gbuf.at[k, h, 1 - core], gall.at[k, core, h], sib)
        gall[k, core, h] = gbuf[k, h, core]

    numbers = {"Z": 0, "Y": 0}
    index = {}
    for k in range(4):
        for h in range(2):
            index[k, h] = numbers[KIND[k][h]]
            numbers[KIND[k][h]] += 1

    def zc(k, h):
        n = index[k, h]
        ready(k, h)

        def term(zb):
            return jnp.dot(hs[pl.ds(2 * zb, 2)].reshape(480, 1024), cs[k, h], preferred_element_type=f32)

        ring_start(("z", n), term, zs1.at[n], zsb.at[n], zr1.at[n], zrb.at[n], zhold.at[n], zown.at[n])

    def zm_(k, h):
        n = index[k, h]
        ring_mid(("z", n), zs2.at[n], zr1.at[n], zr2.at[n], zhold.at[n])

    def ze(k, h):
        n = index[k, h]
        left, right = ring_end(("z", n), zrb.at[n], zr2.at[n], zown.at[n])
        zown[n, :, pl.ds(0, 128)] = left
        zown[n, :, pl.ds(128, 128)] = right
        theirs = pl.ds(pl.multiple_of((1 - y_lo) * 240, 16), 240)
        zys[n] = zown[n, theirs, :].astype(bf16)
        st["zy", n] = send(zys.at[n], zyr.at[n], across)

    def zf_(k, h):
        n = index[k, h]
        st["zy", n].wait_recv()
        mine = pl.ds(pl.multiple_of(y_lo * 240, 16), 240)
        total = zown[n, mine, :] + zyr[n].astype(f32)
        finish(k, h, total[:, :128], total[:, 128:])

    def yc(k, h):
        n = index[k, h]
        ready(k, h)
        for i in range(4):
            hidden(i)

        def body(zb, carry):
            yys[n, zb] = jnp.dot(hs[2 * zb + 1 - y_lo], cs[k, h], preferred_element_type=f32).astype(bf16)
            return carry

        lax.fori_loop(0, 4, body, 0)
        st["yy", n] = send(yys.at[n], yyr.at[n], across)

    def ys(k, h):
        n = index[k, h]
        st["yy", n].wait_recv()

        def term(zb):
            return jnp.dot(hs[2 * zb + y_lo], cs[k, h], preferred_element_type=f32) + yyr[n, zb].astype(f32)

        ring_start(("y", n), term, ys1.at[n], ysb.at[n], yr1.at[n], yrb.at[n], yhold.at[n], yown.at[n])

    def ym(k, h):
        n = index[k, h]
        ring_mid(("y", n), ys2.at[n], yr1.at[n], yr2.at[n], yhold.at[n])

    def ye(k, h):
        n = index[k, h]
        left, right = ring_end(("y", n), yrb.at[n], yr2.at[n], yown.at[n])
        finish(k, h, left, right)

    def ad(k):
        for h in range(2):
            st["g", k, h].wait_recv()
        if k < 3:
            adam_fetch(k + 1)
        row = lax.broadcasted_iota(jnp.int32, (128, 120), 0)
        col = lax.broadcasted_iota(jnp.int32, (128, 120), 1)
        pick = jnp.where(col == (row % 16) * 8 + row // 16, 1.0, 0.0).astype(bf16)
        for b in range(8):
            for i in range(3):
                st["m", k, b, i].wait()
            g = gall[k, b // 4, (b // 2) % 2, :, (b % 2) * 128:(b % 2 + 1) * 128]
            grad[:, b * 512 + k * 128:b * 512 + (k + 1) * 128] = g
            m = adam[k % 2, 0, b]
            one = beta_one * adam[k % 2, 1, b] + (1.0 - beta_one) * g
            two = beta_two * adam[k % 2, 2, b] + (1.0 - beta_two) * g * g
            one_hat = one / (1.0 - beta_one**bias_steps)
            two_hat = two / (1.0 - beta_two**bias_steps)
            new = m - learn_rate * (one_hat / (jnp.sqrt(two_hat) + adam_eps) + decay_rate * m)
            p = jnp.dot(pick, new.astype(bf16), preferred_element_type=f32).astype(bf16)
            wsend[k, :, :, b * 128:(b + 1) * 128] = p.reshape(8, 16, 128)
        st["l", k] = local(wsend.at[k, mp], wbuf.at[k, mp, slot])
        st["a", k] = []
        for (px, py), device in zip(peers, peer_place):
            st["a", k].append(send(wsend.at[k, px * 2 + py], wbuf.at[k, mp, slot], device))

    def ga(k):
        st["l", k].wait()
        for copy in st["a", k]:
            copy.wait_recv()
        mine = wbuf.at[k, :, slot]
        st["u", k] = send(mine, mine, z_up)
        st["d", k] = send(mine, mine, z_down)
        st["s", k] = [send(mine, mine, sib)]

    def gb(k):
        below, above = ((z + 3) % 4) * 2 + core, ((z + 1) % 4) * 2 + core
        st["u", k].wait_recv()
        low = wbuf.at[k, pl.ds(0, 4), below]
        st["ru", k] = send(low, low, z_up)
        st["d", k].wait_recv()
        high = wbuf.at[k, pl.ds(4, 4), above]
        st["rd", k] = send(high, high, z_down)
        for s in (below, above):
            st["s", k].append(send(wbuf.at[k, :, s], wbuf.at[k, :, s], sib))

    def gc(k):
        far = ((z + 2) % 4) * 2 + core
        st["ru", k].wait_recv()
        st["rd", k].wait_recv()
        st["s", k].append(send(wbuf.at[k, :, far], wbuf.at[k, :, far], sib))

    def mm(k):
        for copy in st["s", k]:
            copy.wait_recv()
        if "swap" not in st:
            swap.wait_recv()
            st["swap"] = True
        lhs = abuf[...].reshape(384, 1024)

        def body(n, carry):
            cols = pl.ds(pl.multiple_of(n * 256, 256), 256)
            rhs = wbuf[k, :, :, :, cols].reshape(1024, 256)
            p = jnp.dot(lhs, rhs, preferred_element_type=f32).astype(bf16)
            for i in range(4):
                part[k, n, i] = p[(i % 2) * 192:(i % 2 + 1) * 192, (i // 2) * 128:(i // 2 + 1) * 128]
            return carry

        lax.fori_loop(0, 4, body, 0)
        far, above, below = (x + 2) % 4, (x + 1) % 4, (x + 3) % 4
        lo, hi = pl.ds(0, 2), pl.ds(2, 2)
        st["f1", k] = [send(part.at[k, far, lo], r1.at[k, 0], x_up), send(part.at[k, far, hi], r1.at[k, 1], x_down)]
        st["fb", k] = [send(part.at[k, above, hi], rb.at[k, 0], x_up), send(part.at[k, below, lo], rb.at[k, 1], x_down)]

    def f2(k):
        above, below = (x + 1) % 4, (x + 3) % 4
        st["f1", k][0].wait_recv()
        s2[k, 0] = (part[k, above, pl.ds(0, 2)].astype(f32) + r1[k, 0].astype(f32)).astype(bf16)
        a = send(s2.at[k, 0], r2.at[k, 0], x_up)
        st["f1", k][1].wait_recv()
        s2[k, 1] = (part[k, below, pl.ds(2, 2)].astype(f32) + r1[k, 1].astype(f32)).astype(bf16)
        st["f2", k] = [a, send(s2.at[k, 1], r2.at[k, 1], x_down)]

    def f3(k):
        st["fb", k][1].wait_recv()
        st["f2", k][0].wait_recv()
        q[k, pl.ds(0, 2)] = (part[k, x, pl.ds(0, 2)].astype(f32) + rb[k, 1].astype(f32) + r2[k, 0].astype(f32)).astype(bf16)
        st["fb", k][0].wait_recv()
        st["f2", k][1].wait_recv()
        q[k, pl.ds(2, 2)] = (part[k, x, pl.ds(2, 2)].astype(f32) + rb[k, 0].astype(f32) + r2[k, 1].astype(f32)).astype(bf16)
        st["g", k] = [send(q.at[k, (y + d) % 4], ug.at[k, d - 1], y_place[d - 1]) for d in range(1, 4)]

    def f5(k):
        cols = pl.ds(k * 128, 128)
        total = q[k, y].astype(f32)
        for i in range(3):
            st["g", k][i].wait_recv()
            total = total + ug[k, i].astype(f32)
        attended = att[:, k].reshape(192, 128).astype(bf16).astype(f32)
        stream = (residual[:, cols].astype(f32) + attended).astype(bf16)
        out[:, cols] = (stream.astype(f32) + total).astype(bf16)

    def ap():
        for g in range(HEADS // KV_HEADS):
            qbuf[:, g] = queries[:, :, g * 128:(g + 1) * 128].astype(f32)
        nbuf[0] = keys_new[...].astype(f32)
        nbuf[1] = values_new[...].astype(f32)
        for copy in st["kv"]:
            copy.wait()

    def at(i):
        position = lax.broadcasted_iota(jnp.int32, (16, 128), 1)
        when = lax.broadcasted_iota(jnp.int32, (16, 1), 0) // 4
        heads = HEADS // KV_HEADS

        def rows(n, carry):
            for j in range(4):
                r = i * 8 + n * 4 + j
                qr = jnp.concatenate(
                    [qbuf[t, g, pl.ds(r, 1), :] for t in range(4) for g in range(heads)], axis=0)
                cached = lax.dot_general(qr.astype(bf16), kbuf[r], (((1,), (1,)), ((), ())),
                                         preferred_element_type=f32) * HEAD_DIM ** (-0.5)
                cached = jnp.where(position < lengths[r], cached, -jnp.inf)
                fresh = []
                for s in range(4):
                    score = jnp.sum(qr * nbuf[0, s, pl.ds(r, 1), :], axis=1, keepdims=True) * HEAD_DIM ** (-0.5)
                    fresh.append(jnp.where(when >= s, score, -jnp.inf))
                highest = jnp.max(cached, axis=1, keepdims=True)
                for score in fresh:
                    highest = jnp.maximum(highest, score)
                cached = jnp.exp(cached - highest)
                fresh = [jnp.exp(score - highest) for score in fresh]
                total = jnp.sum(cached, axis=1, keepdims=True) + (fresh[0] + fresh[1]) + (fresh[2] + fresh[3])
                result = jnp.dot((cached / total).astype(bf16), vbuf[r], preferred_element_type=f32)
                for s in range(4):
                    weight = (fresh[s] / total).astype(bf16).astype(f32)
                    result = result + weight * nbuf[1, s, pl.ds(r, 1), :]
                for t in range(4):
                    for g in range(heads):
                        att[t, g, pl.ds(r, 1), :] = result[t * heads + g:t * heads + g + 1]
            return carry

        lax.fori_loop(0, 2, rows, 0)

    steps = {"zc": zc, "zm": zm_, "ze": ze, "zf": zf_, "yc": yc, "ys": ys, "ym": ym, "ye": ye, "ad": ad,
             "ga": ga, "gb": gb, "gc": gc, "mm": mm, "f2": f2, "f3": f3, "f5": f5, "ap": ap, "at": at}
    for name, *where in ORDER:
        steps[name](*where)
    for copy in sends:
        copy.wait_send()


def fused(learn_hidden, out_cot, acts, queries, keys, values, keys_new, values_new, lengths, residual, master, first, second):
    ht = learn_hidden.T.reshape(8, 240, 512)
    kinds = [a for pair in KIND for a in pair]
    nz, ny = max(kinds.count("Z"), 1), max(kinds.count("Y"), 1)

    def ring(n, r):
        return [pltpu.VMEM((n, 2, r, 128), bf16)] * 7 + [pltpu.VMEM((n, r, 256), f32)]

    copies = 4 + 16 + 1 + 8 * 8 + 4 * 24
    locals_ = 4 + 16 + 2 + 4 * (24 + 1)
    return pl.pallas_call(
        fused_kernel,
        out_shape=(jax.ShapeDtypeStruct((192, 512), bf16), jax.ShapeDtypeStruct((120, 4096), f32)),
        in_specs=[pl.BlockSpec(memory_space=pl.ANY)] * 2 + [pl.BlockSpec(memory_space=pltpu.VMEM)] * 2
        + [pl.BlockSpec(memory_space=pl.ANY)] * 2 + [pl.BlockSpec(memory_space=pltpu.VMEM)] * 2
        + [pl.BlockSpec(memory_space=pltpu.SMEM), pl.BlockSpec(memory_space=pltpu.VMEM)]
        + [pl.BlockSpec(memory_space=pl.ANY)] * 3,
        out_specs=(pl.BlockSpec(memory_space=pltpu.VMEM),) * 2,
        scratch_shapes=[
            pltpu.VMEM((8, 240, 1024), bf16),
            pltpu.VMEM((4, 2, 1024, 256), bf16),
            *ring(nz, 480),
            pltpu.VMEM((nz, 240, 256), bf16),
            pltpu.VMEM((nz, 240, 256), bf16),
            pltpu.VMEM((ny, 4, 240, 256), bf16),
            pltpu.VMEM((ny, 4, 240, 256), bf16),
            *ring(ny, 240),
            pltpu.VMEM((4, 2, 2, 120, 256), f32),
            pltpu.VMEM((4, 2, 2, 120, 256), f32),
            pltpu.VMEM((2, 3, 8, 120, 128), f32),
            pltpu.VMEM((4, 8, 16, 1024), bf16),
            pltpu.VMEM((4, 8, 8, 16, 1024), bf16),
            pltpu.VMEM((2, 192, 1024), bf16),
            pltpu.VMEM((2, 192, 1024), bf16),
            pltpu.VMEM((4, 4, 4, 192, 128), bf16),
            *[pltpu.VMEM((4, 2, 2, 192, 128), bf16)] * 4,
            pltpu.VMEM((4, 4, 192, 128), bf16),
            pltpu.VMEM((4, 3, 192, 128), bf16),
            pltpu.VMEM((48, 128, 128), bf16),
            pltpu.VMEM((48, 128, 128), bf16),
            pltpu.VMEM((4, 4, 48, 128), f32),
            pltpu.VMEM((2, 4, 48, 128), f32),
            pltpu.VMEM((4, 4, 48, 128), f32),
            pltpu.SemaphoreType.DMA((locals_,)),
            pltpu.SemaphoreType.DMA((copies,)),
            pltpu.SemaphoreType.DMA((copies,)),
        ],
        compiler_params=pltpu.CompilerParams(collective_id=0, has_side_effects=True, vmem_limit_bytes=60 * 2**20),
        cost_estimate=pl.CostEstimate(flops=11274289152, bytes_accessed=20 * 2**20, transcendentals=0),
        name="fused",
    )(ht, out_cot, acts, queries, keys, values, keys_new, values_new, lengths, residual, master, first, second)


def local(
    learn_hidden,
    out_cot,
    master,
    moment_one,
    moment_two,
    queries,
    keys_cache,
    values_cache,
    keys_new,
    values_new,
    lengths,
    residual,
    unit_acts,
):
    mixed, gradient_rows = fused(
        learn_hidden, out_cot, unit_acts.reshape(192, 1920), queries, keys_cache, values_cache, keys_new, values_new,
        lengths, residual.reshape(192, 512), master, moment_one, moment_two
    )
    mixed = mixed.reshape(residual.shape)
    moment_one_next = beta_one * moment_one + (1.0 - beta_one) * gradient_rows
    moment_two_next = beta_two * moment_two + (1.0 - beta_two) * gradient_rows * gradient_rows
    first_hat = moment_one_next / (1.0 - beta_one**bias_steps)
    second_hat = moment_two_next / (1.0 - beta_two**bias_steps)
    master_next = master - learn_rate * (
        first_hat / (jnp.sqrt(second_hat) + adam_eps) + decay_rate * master
    )
    return (mixed, master_next, moment_one_next, moment_two_next)


def solution(mesh):
    placed = (
        P("dp", "mp"),
        P("dp", None),
        P(("mp", "dp"), None),
        P(("mp", "dp"), None),
        P(("mp", "dp"), None),
        P(None, "dp", "mp"),
        P("dp", None, "mp"),
        P("dp", None, "mp"),
        P(None, "dp", "mp"),
        P(None, "dp", "mp"),
        P("dp"),
        P(None, "dp", "mp"),
        P(None, "dp", "mp", None),
    )
    return jax.shard_map(
        local,
        mesh=mesh,
        in_specs=placed,
        out_specs=(
            P(None, "dp", "mp"),
            P(("mp", "dp"), None),
            P(("mp", "dp"), None),
            P(("mp", "dp"), None),
        ),
        check_vma=False,
    )
```

```python
import functools
import jax
import jax.numpy as jnp
from jax import lax
from jax.experimental import pallas as pl
from jax.experimental.pallas import tpu as pltpu
from jax.sharding import PartitionSpec as P

MESHID = pl.DeviceIdType.MESH
bf16, f32 = jnp.bfloat16, jnp.float32
HEADS = 32
KV_HEADS = 8
HEAD_DIM = 128
CHUNKS = 4
KIND = (("Z", "Z"), ("Z", "B"), ("B", "B"), ("B", "B"))
NEAR = 192
ORDER = [
    ("zc", 0, 1), ("bs", 1, 1), ("bs", 2, 0), ("zc", 1, 0), ("bs", 2, 1), ("hf", 0), ("bs", 3, 1), ("zm", 0, 1),
    ("ac",), ("ap",), ("zm", 1, 0), ("zc", 0, 0), ("ze", 0, 1), ("bf", 1, 1), ("hf", 1), ("hf", 2), ("hf", 3),
    ("zm", 0, 0), ("bf", 2, 0), ("at", 0), ("bz", 1, 1), ("bf", 2, 1), ("bf", 3, 1), ("bs", 3, 0), ("bz", 2, 0),
    ("ze", 0, 0), ("zf", 0, 1), ("ym", 1, 1), ("bz", 2, 1), ("ym", 2, 0), ("bf", 3, 0), ("ze", 1, 0), ("zf", 0, 0),
    ("bz", 3, 1), ("ad", 0), ("ym", 2, 1), ("bz", 3, 0), ("ye", 2, 0), ("ye", 1, 1), ("zf", 1, 0), ("ga", 0),
    ("at", 1), ("ym", 3, 1), ("ye", 2, 1), ("ad", 1), ("ad", 2), ("ym", 3, 0), ("sw",), ("gb", 0), ("ga", 1),
    ("ye", 3, 0), ("gc", 0), ("at", 2), ("ye", 3, 1), ("ga", 2), ("ad", 3), ("gb", 1), ("at", 3), ("mm", 0),
    ("gb", 2), ("f2", 0), ("ga", 3), ("gc", 1), ("mm", 1), ("gc", 2), ("mm", 2), ("f2", 1), ("gb", 3), ("f2", 2),
    ("gc", 3), ("at", 4), ("mm", 3), ("f3", 0), ("at", 5), ("f3", 1), ("f3", 2), ("f5", 0), ("f2", 3), ("f5", 1),
    ("f3", 3), ("f5", 2), ("f5", 3),
]
beta_one = 0.9
beta_two = 0.999
learn_rate = 0.01
decay_rate = 0.1
adam_eps = 1e-08
bias_steps = 10.0


def coords():
    dp, mp = lax.axis_index("dp"), lax.axis_index("mp")
    return dp // 4, (dp // 2) % 2, dp % 2, mp // 2, mp % 2


def place(z, y_lo, core, x, y_hi):
    return ((z * 2 + y_lo) * 2 + core, x * 2 + y_hi)


def fused_kernel(hidden_in, cot, acts, queries, keys, values, keys_new, values_new, lengths, residual,
                 master, first, second, out, grad,
                 hs, cs, zs1, zsb, zs2, zr1, zrb, zr2, zhold, zown, zys, zyr,
                 hraw, ho, co, ys1, ysb, ys2, yr1, yrb, yr2, yhold, yown, gbuf, gall, adam,
                 wsend, wbuf, asend, abuf, part, r1, rb, s2, r2, q, ug, kbuf, vbuf, qbuf, nbuf, att,
                 loc_sem, send_sem, recv_sem):
    z, y_lo, core, x, y_hi = coords()
    y, mp, slot = y_hi * 2 + y_lo, x * 2 + y_hi, z * 2 + core

    def at_y(yy):
        return place(z, yy % 2, core, x, yy // 2)

    sib = place(z, y_lo, 1 - core, x, y_hi)
    z_up, z_down = place((z + 1) % 4, y_lo, core, x, y_hi), place((z + 3) % 4, y_lo, core, x, y_hi)
    x_up, x_down = place(z, y_lo, core, (x + 1) % 4, y_hi), place(z, y_lo, core, (x + 3) % 4, y_hi)
    y_place = [at_y((y + d) % 4) for d in range(1, 4)]
    across = place(z, 1 - y_lo, core, x, y_hi)
    peers = [((x + i // 2) % 4, (y_hi + i % 2) % 2) for i in range(1, 8)]
    peer_place = [place(z, y_lo, core, px, py) for px, py in peers]

    count = [0, 0]
    sends = []
    st = {}

    def send(src, dst, device):
        i = count[0]
        count[0] += 1
        copy = pltpu.make_async_remote_copy(
            src_ref=src, dst_ref=dst, send_sem=send_sem.at[i], recv_sem=recv_sem.at[i],
            device_id=device, device_id_type=MESHID)
        copy.start()
        sends.append(copy)
        return copy

    def local(src, dst):
        i = count[1]
        count[1] += 1
        copy = pltpu.make_async_copy(src, dst, loc_sem.at[i])
        copy.start()
        return copy

    other = at_y((y + 3 + 2 * y_lo) % 4)
    raw = local(hidden_in, hraw)
    barrier = pltpu.get_barrier_semaphore()
    everyone = peer_place + [sib, z_up, z_down, y_place[0], y_place[2]]
    for device in everyone:
        pl.semaphore_signal(barrier, inc=1, device_id=device, device_id_type=MESHID)
    zp, zm, zf = (z + 1) % 4, (z + 3) % 4, (z + 2) % 4
    offset = [2, 1, 3, 0]

    def turn_hidden(i):
        row = lax.broadcasted_iota(jnp.int32, (240, 384), 0)
        lane = lax.broadcasted_iota(jnp.int32, (240, 384), 1)
        for yl in range(2):
            b = ((z + offset[i]) % 4) * 2 + yl
            start = jnp.minimum(b * 240 // 128 * 128, 1536)
            e = jnp.where(lane - (b * 240 - start) == row, 1.0, 0.0).astype(bf16)
            window = hraw[:, pl.ds(pl.multiple_of(start, 128), 384)]
            turned = lax.dot_general(e, window, (((1,), (1,)), ((), ())), preferred_element_type=f32)
            hs[b, :, pl.ds(0, 512)] = turned.astype(bf16)

    def share_hidden(i):
        zb = (z + offset[i]) % 4
        blocks = pl.ds(zb * 2, 2)
        st["h", i] = send(hs.at[blocks, :, pl.ds(0, 512)], hs.at[blocks, :, pl.ds(512, 512)], sib)
        st["hy", i] = send(hs.at[zb * 2 + 1 - y_lo, :, pl.ds(0, 512)], ho.at[i, :, pl.ds(0, 512)], across)

    def hf(i):
        st["hy", i].wait_recv()
        st["hs", i] = send(ho.at[i, :, pl.ds(0, 512)], ho.at[i, :, pl.ds(512, 512)], sib)

    def share_cotangent(k, h):
        st["c", k, h] = []
        for i in range(2):
            mine = pl.ds(pl.multiple_of((4 * core + 2 * h + i) * 512 + k * 128, 128), 128)
            theirs = pl.ds(pl.multiple_of((4 - 4 * core + 2 * h + i) * 512 + k * 128, 128), 128)
            lanes = pl.ds(i * 128, 128)
            st["c", k, h].append(send(cot.at[:, theirs], cs.at[k, h, pl.ds(512, 512), lanes], sib))
            st["c", k, h].append(local(cot.at[:, mine], cs.at[k, h, pl.ds(0, 512), lanes]))

    first_use = [where for name, *where in ORDER if name in ("bs", "zc")]
    raw.wait()
    turn_hidden(0)
    pl.semaphore_wait(barrier, len(everyone))
    share_hidden(0)
    share_cotangent(*first_use[0])
    for i in range(1, 4):
        turn_hidden(i)
        share_hidden(i)
    for where in first_use[1:]:
        share_cotangent(*where)
    st["kv"] = [local(keys, kbuf), local(values, vbuf)]

    def hidden(i):
        if ("got", i) not in st:
            st["got", i] = True
            st["h", i].wait_recv()

    def adam_fetch(k):
        for b in range(8):
            for i, ref in enumerate((master, first, second)):
                st["m", k, b, i] = local(ref.at[:, pl.ds(b * 512 + k * 128, 128)], adam.at[k % 2, i, b])

    adam_fetch(0)

    def ac():
        unit = lax.broadcasted_iota(jnp.int32, (384, 256), 0)
        lane = lax.broadcasted_iota(jnp.int32, (384, 256), 1)
        owner = (lane % 128) // 16
        target = ((owner // 2) * 4 + (lane // 128) * 2 + owner % 2) * 15 + lane % 16
        target = jnp.where(lane % 16 < 15, target, -1000)
        for b in range(8):
            start, shift = (b * 240) // 128 * 128, (b * 240) % 128
            depth = 256 if shift + 240 <= 256 else 384
            e = jnp.where(unit[:depth] - shift == target[:depth], 1.0, 0.0).astype(bf16)
            a = jnp.dot(acts[:, start:start + depth], e, preferred_element_type=f32).astype(bf16)
            asend[0, :, b * 128:(b + 1) * 128] = a[:, :128]
            asend[1, :, b * 128:(b + 1) * 128] = a[:, 128:]
        abuf[y_lo] = asend[y_lo]

    def sw():
        st["sw"] = send(asend.at[1 - y_lo], abuf.at[y_lo], across)

    def ready(k, h):
        for i in range(2):
            st["c", k, h][2 * i].wait_recv()
            st["c", k, h][2 * i + 1].wait()

    def ring_start(key, term, s1, sb, r1, rb, hold, own):
        hidden(0)
        p = term(0, zf)
        s1[0] = p[:, :128].astype(bf16)
        s1[1] = p[:, 128:].astype(bf16)
        st["r1", key] = [send(s1.at[0], r1.at[0], z_up), send(s1.at[1], r1.at[1], z_down)]
        hidden(1)
        p = term(1, zp)
        sb[0] = p[:, 128:].astype(bf16)
        b0 = send(sb.at[0], rb.at[0], z_up)
        hold[0] = p[:, :128].astype(hold.dtype)
        hidden(2)
        p = term(2, zm)
        sb[1] = p[:, :128].astype(bf16)
        b1 = send(sb.at[1], rb.at[1], z_down)
        hold[1] = p[:, 128:].astype(hold.dtype)
        st["rb", key] = [b0, b1]
        hidden(3)
        own[...] = term(3, z)

    def ring_mid(key, s2, r1, r2, hold):
        st["r2", key] = []
        for d, device in ((0, z_up), (1, z_down)):
            st["r1", key][d].wait_recv()
            s2[d] = (hold[d].astype(f32) + r1[d].astype(f32)).astype(bf16)
            st["r2", key].append(send(s2.at[d], r2.at[d], device))

    def ring_end(key, rb, r2, own):
        st["rb", key][1].wait_recv()
        st["r2", key][0].wait_recv()
        left = own[:, :128] + rb[1].astype(f32) + r2[0].astype(f32)
        st["rb", key][0].wait_recv()
        st["r2", key][1].wait_recv()
        right = own[:, 128:] + rb[0].astype(f32) + r2[1].astype(f32)
        return left, right

    def finish(k, h, left, right):
        gbuf[k, h, :, :, pl.ds(0, 128)] = left.reshape(2, 120, 128)
        gbuf[k, h, :, :, pl.ds(128, 128)] = right.reshape(2, 120, 128)
        st["g", k, h] = send(gbuf.at[k, h, 1 - core], gall.at[k, core, h], sib)
        gall[k, core, h] = gbuf[k, h, core]

    numbers = {"Z": 0, "B": 0}
    index = {}
    for k in range(4):
        for h in range(2):
            index[k, h] = numbers[KIND[k][h]]
            numbers[KIND[k][h]] += 1

    def zc(k, h):
        n = index[k, h]
        ready(k, h)

        def term(i, zb):
            return jnp.dot(hs[pl.ds(2 * zb, 2)].reshape(480, 1024), cs[k, h], preferred_element_type=f32)

        ring_start(("z", n), term, zs1.at[n], zsb.at[n], zr1.at[n], zrb.at[n], zhold.at[n], zown.at[n])

    def zm_(k, h):
        n = index[k, h]
        ring_mid(("z", n), zs2.at[n], zr1.at[n], zr2.at[n], zhold.at[n])

    def ze(k, h):
        n = index[k, h]
        left, right = ring_end(("z", n), zrb.at[n], zr2.at[n], zown.at[n])
        zown[n, :, pl.ds(0, 128)] = left
        zown[n, :, pl.ds(128, 128)] = right
        theirs = pl.ds(pl.multiple_of((1 - y_lo) * 240, 16), 240)
        zys[n] = zown[n, theirs, :].astype(bf16)
        st["zy", n] = send(zys.at[n], zyr.at[n], across)

    def zf_(k, h):
        n = index[k, h]
        st["zy", n].wait_recv()
        mine = pl.ds(pl.multiple_of(y_lo * 240, 16), 240)
        total = zown[n, mine, :] + zyr[n].astype(f32)
        finish(k, h, total[:, :128], total[:, 128:])

    def bs(k, h):
        n = index[k, h]
        ready(k, h)
        base = (x % 2) * 512
        near = pl.ds(pl.multiple_of(base, 16), NEAR)
        rest = pl.ds(pl.multiple_of(base + NEAR, 16), 512 - NEAR)
        st["by", n] = [send(cs.at[k, h, near], co.at[n, near], across), send(cs.at[k, h, rest], co.at[n, rest], other)]

    def bf(k, h):
        n = index[k, h]
        for copy in st["by", n]:
            copy.wait_recv()
        base = (x % 2) * 512
        low, high = pl.ds(pl.multiple_of(base, 16), 256), pl.ds(pl.multiple_of(base + 256, 16), 256)
        st["bx", n] = [send(co.at[n, low], co.at[n, low], x_up), send(co.at[n, high], co.at[n, high], x_down)]

    def bz(k, h):
        n = index[k, h]
        for copy in st["bx", n]:
            copy.wait_recv()

        def term(i, zb):
            if ("far", i) not in st:
                st["far", i] = True
                st["hs", i].wait_recv()
            return (jnp.dot(hs[2 * zb + y_lo], cs[k, h], preferred_element_type=f32)
                    + jnp.dot(ho[i], co[n], preferred_element_type=f32))

        ring_start(("y", n), term, ys1.at[n], ysb.at[n], yr1.at[n], yrb.at[n], yhold.at[n], yown.at[n])

    def ym(k, h):
        n = index[k, h]
        ring_mid(("y", n), ys2.at[n], yr1.at[n], yr2.at[n], yhold.at[n])

    def ye(k, h):
        n = index[k, h]
        left, right = ring_end(("y", n), yrb.at[n], yr2.at[n], yown.at[n])
        finish(k, h, left, right)

    def ad(k):
        for h in range(2):
            st["g", k, h].wait_recv()
        if k < 3:
            adam_fetch(k + 1)
        row = lax.broadcasted_iota(jnp.int32, (128, 120), 0)
        col = lax.broadcasted_iota(jnp.int32, (128, 120), 1)
        pick = jnp.where(col == (row % 16) * 8 + row // 16, 1.0, 0.0).astype(bf16)
        for b in range(8):
            for i in range(3):
                st["m", k, b, i].wait()
            g = gall[k, b // 4, (b // 2) % 2, :, (b % 2) * 128:(b % 2 + 1) * 128]
            grad[:, b * 512 + k * 128:b * 512 + (k + 1) * 128] = g
            m = adam[k % 2, 0, b]
            one = beta_one * adam[k % 2, 1, b] + (1.0 - beta_one) * g
            two = beta_two * adam[k % 2, 2, b] + (1.0 - beta_two) * g * g
            one_hat = one / (1.0 - beta_one**bias_steps)
            two_hat = two / (1.0 - beta_two**bias_steps)
            new = m - learn_rate * (one_hat / (jnp.sqrt(two_hat) + adam_eps) + decay_rate * m)
            p = jnp.dot(pick, new.astype(bf16), preferred_element_type=f32).astype(bf16)
            wsend[k, :, :, b * 128:(b + 1) * 128] = p.reshape(8, 16, 128)
        st["l", k] = local(wsend.at[k, mp], wbuf.at[k, mp, slot])
        st["a", k] = []
        for (px, py), device in zip(peers, peer_place):
            st["a", k].append(send(wsend.at[k, px * 2 + py], wbuf.at[k, mp, slot], device))

    def ga(k):
        st["l", k].wait()
        for copy in st["a", k]:
            copy.wait_recv()
        mine = wbuf.at[k, :, slot]
        st["u", k] = send(mine, mine, z_up)
        st["d", k] = send(mine, mine, z_down)
        st["s", k] = [send(mine, mine, sib)]

    def gb(k):
        below, above = ((z + 3) % 4) * 2 + core, ((z + 1) % 4) * 2 + core
        st["u", k].wait_recv()
        low = wbuf.at[k, pl.ds(0, 4), below]
        st["ru", k] = send(low, low, z_up)
        st["d", k].wait_recv()
        high = wbuf.at[k, pl.ds(4, 4), above]
        st["rd", k] = send(high, high, z_down)
        for s in (below, above):
            st["s", k].append(send(wbuf.at[k, :, s], wbuf.at[k, :, s], sib))

    def gc(k):
        far = ((z + 2) % 4) * 2 + core
        st["ru", k].wait_recv()
        st["rd", k].wait_recv()
        st["s", k].append(send(wbuf.at[k, :, far], wbuf.at[k, :, far], sib))

    def mm(k):
        for copy in st["s", k]:
            copy.wait_recv()
        if "swap" not in st:
            st["sw"].wait_recv()
            st["swap"] = True
        lhs = abuf[...].reshape(384, 1024)

        def body(n, carry):
            cols = pl.ds(pl.multiple_of(n * 256, 256), 256)
            rhs = wbuf[k, :, :, :, cols].reshape(1024, 256)
            p = jnp.dot(lhs, rhs, preferred_element_type=f32).astype(bf16)
            for i in range(4):
                part[k, n, i] = p[(i % 2) * 192:(i % 2 + 1) * 192, (i // 2) * 128:(i // 2 + 1) * 128]
            return carry

        lax.fori_loop(0, 4, body, 0)
        far, above, below = (x + 2) % 4, (x + 1) % 4, (x + 3) % 4
        lo, hi = pl.ds(0, 2), pl.ds(2, 2)
        st["f1", k] = [send(part.at[k, far, lo], r1.at[k, 0], x_up), send(part.at[k, far, hi], r1.at[k, 1], x_down)]
        st["fb", k] = [send(part.at[k, above, hi], rb.at[k, 0], x_up), send(part.at[k, below, lo], rb.at[k, 1], x_down)]

    def f2(k):
        above, below = (x + 1) % 4, (x + 3) % 4
        st["f1", k][0].wait_recv()
        s2[k, 0] = (part[k, above, pl.ds(0, 2)].astype(f32) + r1[k, 0].astype(f32)).astype(bf16)
        a = send(s2.at[k, 0], r2.at[k, 0], x_up)
        st["f1", k][1].wait_recv()
        s2[k, 1] = (part[k, below, pl.ds(2, 2)].astype(f32) + r1[k, 1].astype(f32)).astype(bf16)
        st["f2", k] = [a, send(s2.at[k, 1], r2.at[k, 1], x_down)]

    def f3(k):
        st["fb", k][1].wait_recv()
        st["f2", k][0].wait_recv()
        q[k, pl.ds(0, 2)] = (part[k, x, pl.ds(0, 2)].astype(f32) + rb[k, 1].astype(f32) + r2[k, 0].astype(f32)).astype(bf16)
        st["fb", k][0].wait_recv()
        st["f2", k][1].wait_recv()
        q[k, pl.ds(2, 2)] = (part[k, x, pl.ds(2, 2)].astype(f32) + rb[k, 0].astype(f32) + r2[k, 1].astype(f32)).astype(bf16)
        st["g", k] = [send(q.at[k, (y + d) % 4], ug.at[k, d - 1], y_place[d - 1]) for d in range(1, 4)]

    def f5(k):
        cols = pl.ds(k * 128, 128)
        total = q[k, y].astype(f32)
        for i in range(3):
            st["g", k][i].wait_recv()
            total = total + ug[k, i].astype(f32)
        attended = att[:, k].reshape(192, 128).astype(bf16).astype(f32)
        stream = (residual[:, cols].astype(f32) + attended).astype(bf16)
        out[:, cols] = (stream.astype(f32) + total).astype(bf16)

    def ap():
        for g in range(HEADS // KV_HEADS):
            qbuf[:, g] = queries[:, :, g * 128:(g + 1) * 128].astype(f32)
        nbuf[0] = keys_new[...].astype(f32)
        nbuf[1] = values_new[...].astype(f32)
        for copy in st["kv"]:
            copy.wait()

    def at(i):
        position = lax.broadcasted_iota(jnp.int32, (16, 128), 1)
        when = lax.broadcasted_iota(jnp.int32, (16, 1), 0) // 4
        heads = HEADS // KV_HEADS

        def rows(n, carry):
            for j in range(4):
                r = i * 8 + n * 4 + j
                qr = jnp.concatenate(
                    [qbuf[t, g, pl.ds(r, 1), :] for t in range(4) for g in range(heads)], axis=0)
                cached = lax.dot_general(qr.astype(bf16), kbuf[r], (((1,), (1,)), ((), ())),
                                         preferred_element_type=f32) * HEAD_DIM ** (-0.5)
                cached = jnp.where(position < lengths[r], cached, -jnp.inf)
                fresh = []
                for s in range(4):
                    score = jnp.sum(qr * nbuf[0, s, pl.ds(r, 1), :], axis=1, keepdims=True) * HEAD_DIM ** (-0.5)
                    fresh.append(jnp.where(when >= s, score, -jnp.inf))
                highest = jnp.max(cached, axis=1, keepdims=True)
                for score in fresh:
                    highest = jnp.maximum(highest, score)
                cached = jnp.exp(cached - highest)
                fresh = [jnp.exp(score - highest) for score in fresh]
                total = jnp.sum(cached, axis=1, keepdims=True) + (fresh[0] + fresh[1]) + (fresh[2] + fresh[3])
                result = jnp.dot((cached / total).astype(bf16), vbuf[r], preferred_element_type=f32)
                for s in range(4):
                    weight = (fresh[s] / total).astype(bf16).astype(f32)
                    result = result + weight * nbuf[1, s, pl.ds(r, 1), :]
                for t in range(4):
                    for g in range(heads):
                        att[t, g, pl.ds(r, 1), :] = result[t * heads + g:t * heads + g + 1]
            return carry

        lax.fori_loop(0, 2, rows, 0)

    steps = {"zc": zc, "zm": zm_, "ze": ze, "zf": zf_, "hf": hf, "bs": bs, "bf": bf, "bz": bz, "ac": ac, "sw": sw, "ym": ym, "ye": ye, "ad": ad,
             "ga": ga, "gb": gb, "gc": gc, "mm": mm, "f2": f2, "f3": f3, "f5": f5, "ap": ap, "at": at}
    for name, *where in ORDER:
        steps[name](*where)
    for copy in sends:
        copy.wait_send()


def fused(learn_hidden, out_cot, acts, queries, keys, values, keys_new, values_new, lengths, residual, master, first, second):
    kinds = [a for pair in KIND for a in pair]
    nz, ny = max(kinds.count("Z"), 1), max(kinds.count("B"), 1)

    def ring(n, r):
        return [pltpu.VMEM((n, 2, r, 128), bf16)] * 7 + [pltpu.VMEM((n, r, 256), f32)]

    copies = 12 + 16 + 1 + 8 * 10 + 4 * 24
    locals_ = 4 + 16 + 2 + 4 * (24 + 1)
    return pl.pallas_call(
        fused_kernel,
        out_shape=(jax.ShapeDtypeStruct((192, 512), bf16), jax.ShapeDtypeStruct((120, 4096), f32)),
        in_specs=[pl.BlockSpec(memory_space=pl.ANY)] * 2 + [pl.BlockSpec(memory_space=pltpu.VMEM)] * 2
        + [pl.BlockSpec(memory_space=pl.ANY)] * 2 + [pl.BlockSpec(memory_space=pltpu.VMEM)] * 2
        + [pl.BlockSpec(memory_space=pltpu.SMEM), pl.BlockSpec(memory_space=pltpu.VMEM)]
        + [pl.BlockSpec(memory_space=pl.ANY)] * 3,
        out_specs=(pl.BlockSpec(memory_space=pltpu.VMEM),) * 2,
        scratch_shapes=[
            pltpu.VMEM((8, 240, 1024), bf16),
            pltpu.VMEM((4, 2, 1024, 256), bf16),
            *ring(nz, 480),
            pltpu.VMEM((nz, 240, 256), bf16),
            pltpu.VMEM((nz, 240, 256), bf16),
            pltpu.VMEM((512, 1920), bf16),
            pltpu.VMEM((4, 240, 1024), bf16),
            pltpu.VMEM((ny, 1024, 256), bf16),
            *ring(ny, 240),
            pltpu.VMEM((4, 2, 2, 120, 256), f32),
            pltpu.VMEM((4, 2, 2, 120, 256), f32),
            pltpu.VMEM((2, 3, 8, 120, 128), f32),
            pltpu.VMEM((4, 8, 16, 1024), bf16),
            pltpu.VMEM((4, 8, 8, 16, 1024), bf16),
            pltpu.VMEM((2, 192, 1024), bf16),
            pltpu.VMEM((2, 192, 1024), bf16),
            pltpu.VMEM((4, 4, 4, 192, 128), bf16),
            *[pltpu.VMEM((4, 2, 2, 192, 128), bf16)] * 4,
            pltpu.VMEM((4, 4, 192, 128), bf16),
            pltpu.VMEM((4, 3, 192, 128), bf16),
            pltpu.VMEM((48, 128, 128), bf16),
            pltpu.VMEM((48, 128, 128), bf16),
            pltpu.VMEM((4, 4, 48, 128), f32),
            pltpu.VMEM((2, 4, 48, 128), f32),
            pltpu.VMEM((4, 4, 48, 128), f32),
            pltpu.SemaphoreType.DMA((locals_,)),
            pltpu.SemaphoreType.DMA((copies,)),
            pltpu.SemaphoreType.DMA((copies,)),
        ],
        compiler_params=pltpu.CompilerParams(collective_id=0, has_side_effects=True, vmem_limit_bytes=60 * 2**20),
        cost_estimate=pl.CostEstimate(flops=11274289152, bytes_accessed=20 * 2**20, transcendentals=0),
        name="fused",
    )(learn_hidden, out_cot, acts, queries, keys, values, keys_new, values_new, lengths, residual, master, first, second)


def local(
    learn_hidden,
    out_cot,
    master,
    moment_one,
    moment_two,
    queries,
    keys_cache,
    values_cache,
    keys_new,
    values_new,
    lengths,
    residual,
    unit_acts,
):
    mixed, gradient_rows = fused(
        learn_hidden, out_cot, unit_acts.reshape(192, 1920), queries, keys_cache, values_cache, keys_new, values_new,
        lengths, residual.reshape(192, 512), master, moment_one, moment_two
    )
    mixed = mixed.reshape(residual.shape)
    moment_one_next = beta_one * moment_one + (1.0 - beta_one) * gradient_rows
    moment_two_next = beta_two * moment_two + (1.0 - beta_two) * gradient_rows * gradient_rows
    first_hat = moment_one_next / (1.0 - beta_one**bias_steps)
    second_hat = moment_two_next / (1.0 - beta_two**bias_steps)
    master_next = master - learn_rate * (
        first_hat / (jnp.sqrt(second_hat) + adam_eps) + decay_rate * master
    )
    return (mixed, master_next, moment_one_next, moment_two_next)


def solution(mesh):
    placed = (
        P("dp", "mp"),
        P("dp", None),
        P(("mp", "dp"), None),
        P(("mp", "dp"), None),
        P(("mp", "dp"), None),
        P(None, "dp", "mp"),
        P("dp", None, "mp"),
        P("dp", None, "mp"),
        P(None, "dp", "mp"),
        P(None, "dp", "mp"),
        P("dp"),
        P(None, "dp", "mp"),
        P(None, "dp", "mp", None),
    )
    return jax.shard_map(
        local,
        mesh=mesh,
        in_specs=placed,
        out_specs=(
            P(None, "dp", "mp"),
            P(("mp", "dp"), None),
            P(("mp", "dp"), None),
            P(("mp", "dp"), None),
        ),
        check_vma=False,
    )
```

```python
import functools
import jax
import jax.numpy as jnp
from jax import lax
from jax.experimental import pallas as pl
from jax.experimental.pallas import tpu as pltpu
from jax.sharding import PartitionSpec as P

MESHID = pl.DeviceIdType.MESH
bf16, f32 = jnp.bfloat16, jnp.float32
HEADS = 32
KV_HEADS = 8
HEAD_DIM = 128
CHUNKS = 4
KIND = (("Z", "Z"), ("Z", "B"), ("B", "B"), ("B", "B"))
NEAR = (0, 0, 192, 256, 320)
ORDER = [
    ("za", 0, 0), ("bs", 1, 1), ("ap",), ("za", 1, 0), ("za", 0, 1), ("zb", 0, 0), ("zm", 0, 0), ("zb", 1, 0),
    ("hf", 0), ("bs", 2, 0), ("zc", 0, 0), ("at", 0), ("bs", 2, 1), ("bf", 1, 1), ("at", 1), ("hf", 1), ("bs", 3, 1),
    ("hf", 2), ("bf", 2, 0), ("zb", 0, 1), ("zm", 1, 0), ("at", 2), ("zc", 0, 1), ("ya", 2, 0), ("ya", 1, 1),
    ("hf", 3), ("ac",), ("zm", 0, 1), ("bs", 3, 0), ("bf", 2, 1), ("yb", 1, 1), ("yb", 2, 0), ("ze", 0, 0),
    ("bf", 3, 1), ("ym", 1, 1), ("zc", 1, 0), ("ze", 0, 1), ("ya", 2, 1), ("bf", 3, 0), ("ze", 1, 0), ("ya", 3, 1),
    ("yc", 2, 0), ("yb", 2, 1), ("ym", 2, 0), ("yc", 1, 1), ("yb", 3, 1), ("ya", 3, 0), ("zf", 0, 0), ("zf", 0, 1),
    ("ym", 2, 1), ("ye", 1, 1), ("yb", 3, 0), ("ad", 0), ("yc", 2, 1), ("zf", 1, 0), ("ym", 3, 1), ("yc", 3, 1),
    ("ym", 3, 0), ("ad", 1), ("ga", 0), ("ye", 2, 1), ("yc", 3, 0), ("ye", 2, 0), ("ye", 3, 0), ("sw",), ("ad", 2),
    ("ga", 1), ("at", 3), ("ye", 3, 1), ("gb", 0), ("ad", 3), ("gb", 1), ("gc", 0), ("ga", 2), ("gc", 1), ("mm", 0),
    ("mm", 1), ("ga", 3), ("f2", 0), ("gb", 2), ("f2", 1), ("at", 4), ("gb", 3), ("at", 5), ("f3", 0), ("gc", 2),
    ("f3", 1), ("gc", 3), ("mm", 2), ("mm", 3), ("f2", 2), ("f2", 3), ("f5", 1), ("f5", 0), ("f3", 2), ("f3", 3),
    ("f5", 2), ("f5", 3),
]
beta_one = 0.9
beta_two = 0.999
learn_rate = 0.01
decay_rate = 0.1
adam_eps = 1e-08
bias_steps = 10.0


def coords():
    dp, mp = lax.axis_index("dp"), lax.axis_index("mp")
    return dp // 4, (dp // 2) % 2, dp % 2, mp // 2, mp % 2


def place(z, y_lo, core, x, y_hi):
    return ((z * 2 + y_lo) * 2 + core, x * 2 + y_hi)


def fused_kernel(hidden_in, cot, acts, queries, keys, values, keys_new, values_new, lengths, residual,
                 master, first, second, out, grad,
                 hs, cs, zs1, zsb, zs2, zr1, zrb, zr2, zhold, zown, zys, zyr,
                 hraw, ho, co, ys1, ysb, ys2, yr1, yrb, yr2, yhold, yown, gbuf, adam,
                 wsend, wbuf, asend, abuf, part, r1, rb, s2, r2, q, ug, kbuf, vbuf, qbuf, nbuf, att,
                 loc_sem, send_sem, recv_sem):
    z, y_lo, core, x, y_hi = coords()
    y, mp, slot = y_hi * 2 + y_lo, x * 2 + y_hi, z * 2 + core

    def at_y(yy):
        return place(z, yy % 2, core, x, yy // 2)

    sib = place(z, y_lo, 1 - core, x, y_hi)
    z_up, z_down = place((z + 1) % 4, y_lo, core, x, y_hi), place((z + 3) % 4, y_lo, core, x, y_hi)
    y_place = [at_y((y + d) % 4) for d in range(1, 4)]
    x_place = [place(z, y_lo, core, (x + d) % 4, y_hi) for d in range(1, 4)]
    axes = ((x, x_place[0], x_place[2]), (y, y_place[0], y_place[2]))
    across = place(z, 1 - y_lo, core, x, y_hi)
    peers = [((x + i // 2) % 4, (y_hi + i % 2) % 2) for i in range(1, 8)]
    peer_place = [place(z, y_lo, core, px, py) for px, py in peers]

    count = [0, 0]
    sends = []
    st = {}

    def send(src, dst, device):
        i = count[0]
        count[0] += 1
        copy = pltpu.make_async_remote_copy(
            src_ref=src, dst_ref=dst, send_sem=send_sem.at[i], recv_sem=recv_sem.at[i],
            device_id=device, device_id_type=MESHID)
        copy.start()
        sends.append(copy)
        return copy

    def local(src, dst):
        i = count[1]
        count[1] += 1
        copy = pltpu.make_async_copy(src, dst, loc_sem.at[i])
        copy.start()
        return copy

    other = at_y((y + 3 + 2 * y_lo) % 4)
    raw = local(hidden_in, hraw)
    barrier = pltpu.get_barrier_semaphore()
    everyone = peer_place + [sib, z_up, z_down, y_place[0], y_place[2]]
    for device in everyone:
        pl.semaphore_signal(barrier, inc=1, device_id=device, device_id_type=MESHID)
    zp, zm, zf = (z + 1) % 4, (z + 3) % 4, (z + 2) % 4
    offset = [2, 1, 3, 0]

    def turn_hidden(i):
        row = lax.broadcasted_iota(jnp.int32, (240, 384), 0)
        lane = lax.broadcasted_iota(jnp.int32, (240, 384), 1)
        for yl in range(2):
            b = ((z + offset[i]) % 4) * 2 + yl
            start = jnp.minimum(b * 240 // 128 * 128, 1536)
            e = jnp.where(lane - (b * 240 - start) == row, 1.0, 0.0).astype(bf16)
            window = hraw[:, pl.ds(pl.multiple_of(start, 128), 384)]
            turned = lax.dot_general(e, window, (((1,), (1,)), ((), ())), preferred_element_type=f32)
            hs[b, :, pl.ds(0, 512)] = turned.astype(bf16)

    def share_hidden(i):
        zb = (z + offset[i]) % 4
        blocks = pl.ds(zb * 2, 2)
        st["h", i] = send(hs.at[blocks, :, pl.ds(0, 512)], hs.at[blocks, :, pl.ds(512, 512)], sib)
        st["hy", i] = send(hs.at[zb * 2 + 1 - y_lo, :, pl.ds(0, 512)], ho.at[i, :, pl.ds(0, 512)], across)

    def hf(i):
        st["hy", i].wait_recv()
        st["hs", i] = send(ho.at[i, :, pl.ds(0, 512)], ho.at[i, :, pl.ds(512, 512)], sib)

    def share_cotangent(k, h):
        st["c", k, h] = []
        for i in range(2):
            mine = pl.ds(pl.multiple_of((4 * core + 2 * h + i) * 512 + k * 128, 128), 128)
            theirs = pl.ds(pl.multiple_of((4 - 4 * core + 2 * h + i) * 512 + k * 128, 128), 128)
            lanes = pl.ds(i * 128, 128)
            st["c", k, h].append(send(cot.at[:, theirs], cs.at[k, h, pl.ds(512, 512), lanes], sib))
            st["c", k, h].append(local(cot.at[:, mine], cs.at[k, h, pl.ds(0, 512), lanes]))

    first_use = [where for name, *where in ORDER if name in ("bs", "za")]
    raw.wait()
    turn_hidden(0)
    pl.semaphore_wait(barrier, len(everyone))
    share_hidden(0)
    share_cotangent(*first_use[0])
    for i in range(1, 4):
        turn_hidden(i)
        share_hidden(i)
    for where in first_use[1:]:
        share_cotangent(*where)

    def cache_fetch(i):
        rows = pl.ds(i * 8, 8)
        st["kv", i] = [local(keys.at[rows], kbuf.at[i % 2]), local(values.at[rows], vbuf.at[i % 2])]

    cache_fetch(0)

    def hidden(i):
        if ("got", i) not in st:
            st["got", i] = True
            st["h", i].wait_recv()

    def adam_fetch(k):
        for b in range(8):
            for i, ref in enumerate((master, first, second)):
                st["m", k, b, i] = local(ref.at[:, pl.ds(b * 512 + k * 128, 128)], adam.at[k % 2, i, b])

    adam_fetch(0)

    def ac():
        unit = lax.broadcasted_iota(jnp.int32, (384, 256), 0)
        lane = lax.broadcasted_iota(jnp.int32, (384, 256), 1)
        owner = (lane % 128) // 16
        target = ((owner // 2) * 4 + (lane // 128) * 2 + owner % 2) * 15 + lane % 16
        target = jnp.where(lane % 16 < 15, target, -1000)
        for b in range(8):
            start, shift = (b * 240) // 128 * 128, (b * 240) % 128
            depth = 256 if shift + 240 <= 256 else 384
            e = jnp.where(unit[:depth] - shift == target[:depth], 1.0, 0.0).astype(bf16)
            a = jnp.dot(acts[:, start:start + depth], e, preferred_element_type=f32).astype(bf16)
            asend[0, :, b * 128:(b + 1) * 128] = a[:, :128]
            asend[1, :, b * 128:(b + 1) * 128] = a[:, 128:]
        abuf[y_lo] = asend[y_lo]

    def sw():
        st["sw"] = send(asend.at[1 - y_lo], abuf.at[y_lo], across)

    def ready(k, h):
        for i in range(2):
            st["c", k, h][2 * i].wait_recv()
            st["c", k, h][2 * i + 1].wait()

    def ring_a(key, term, s1, r1):
        hidden(0)
        p = term(0, zf)
        s1[0] = p[:, :128].astype(bf16)
        s1[1] = p[:, 128:].astype(bf16)
        st["r1", key] = [send(s1.at[0], r1.at[0], z_up), send(s1.at[1], r1.at[1], z_down)]

    def ring_b(key, term, sb, rb, hold):
        hidden(1)
        p = term(1, zp)
        sb[0] = p[:, 128:].astype(bf16)
        b0 = send(sb.at[0], rb.at[0], z_up)
        hold[0] = p[:, :128].astype(hold.dtype)
        hidden(2)
        p = term(2, zm)
        sb[1] = p[:, :128].astype(bf16)
        b1 = send(sb.at[1], rb.at[1], z_down)
        hold[1] = p[:, 128:].astype(hold.dtype)
        st["rb", key] = [b0, b1]

    def ring_c(term, own):
        hidden(3)
        own[...] = term(3, z)

    def ring_mid(key, s2, r1, r2, hold):
        st["r2", key] = []
        for d, device in ((0, z_up), (1, z_down)):
            st["r1", key][d].wait_recv()
            s2[d] = (hold[d].astype(f32) + r1[d].astype(f32)).astype(bf16)
            st["r2", key].append(send(s2.at[d], r2.at[d], device))

    def ring_end(key, rb, r2, own):
        st["rb", key][1].wait_recv()
        st["r2", key][0].wait_recv()
        left = own[:, :128] + rb[1].astype(f32) + r2[0].astype(f32)
        st["rb", key][0].wait_recv()
        st["r2", key][1].wait_recv()
        right = own[:, 128:] + rb[0].astype(f32) + r2[1].astype(f32)
        return left, right

    def finish(k, h, left, right):
        for copy in st.get(("g", k - 2, h), []):
            copy.wait_send()
            sends[:] = [c for c in sends if c is not copy]
        st["g", k, h] = []
        for i, half in enumerate((left, right)):
            gbuf[k % 2, h, i] = half.reshape(2, 120, 128)
            cols = pl.ds(pl.multiple_of((4 * core + 2 * h + i) * 512 + k * 128, 128), 128)
            st["g", k, h].append(send(gbuf.at[k % 2, h, i, 1 - core], grad.at[:, cols], sib))
            grad[:, cols] = gbuf[k % 2, h, i, core]

    numbers = {"Z": 0, "B": 0}
    index = {}
    for k in range(4):
        for h in range(2):
            index[k, h] = numbers[KIND[k][h]]
            numbers[KIND[k][h]] += 1

    def zterm(k, h):
        def term(i, zb):
            return jnp.dot(hs[pl.ds(2 * zb, 2)].reshape(480, 1024), cs[k, h], preferred_element_type=f32)

        return term

    def za(k, h):
        n = index[k, h]
        ready(k, h)
        ring_a(("z", n), zterm(k, h), zs1.at[n], zr1.at[n])

    def zb_(k, h):
        n = index[k, h]
        ring_b(("z", n), zterm(k, h), zsb.at[n], zrb.at[n], zhold.at[n])

    def zc(k, h):
        ring_c(zterm(k, h), zown.at[index[k, h]])

    def zm_(k, h):
        n = index[k, h]
        ring_mid(("z", n), zs2.at[n], zr1.at[n], zr2.at[n], zhold.at[n])

    def ze(k, h):
        n = index[k, h]
        left, right = ring_end(("z", n), zrb.at[n], zr2.at[n], zown.at[n])
        zown[n, :, pl.ds(0, 128)] = left
        zown[n, :, pl.ds(128, 128)] = right
        theirs = pl.ds(pl.multiple_of((1 - y_lo) * 240, 16), 240)
        zys[n] = zown[n, theirs, :].astype(bf16)
        st["zy", n] = send(zys.at[n], zyr.at[n], across)

    def zf_(k, h):
        n = index[k, h]
        st["zy", n].wait_recv()
        mine = pl.ds(pl.multiple_of(y_lo * 240, 16), 240)
        total = zown[n, mine, :] + zyr[n].astype(f32)
        finish(k, h, total[:, :128], total[:, 128:])

    def bs(k, h):
        n = index[k, h]
        ready(k, h)
        base = (x % 2) * 512
        few = NEAR[n]
        rest = pl.ds(pl.multiple_of(base + few, 16), 512 - few)
        st["by", n] = [send(cs.at[k, h, rest], co.at[n, rest], other)]
        if few > 0:
            near = pl.ds(pl.multiple_of(base, 16), few)
            st["by", n].append(send(cs.at[k, h, near], co.at[n, near], across))

    def bf(k, h):
        n = index[k, h]
        for copy in st["by", n]:
            copy.wait_recv()
        base = (x % 2) * 512
        low, high = pl.ds(pl.multiple_of(base, 16), 256), pl.ds(pl.multiple_of(base + 256, 16), 256)
        st["bx", n] = [send(co.at[n, low], co.at[n, low], x_place[0]), send(co.at[n, high], co.at[n, high], x_place[2])]

    def bterm(k, h):
        n = index[k, h]

        def term(i, zb):
            if ("far", i) not in st:
                st["far", i] = True
                st["hs", i].wait_recv()
            return (jnp.dot(hs[2 * zb + y_lo], cs[k, h], preferred_element_type=f32)
                    + jnp.dot(ho[i], co[n], preferred_element_type=f32))

        return term

    def ya(k, h):
        n = index[k, h]
        for copy in st["bx", n]:
            copy.wait_recv()
        ring_a(("y", n), bterm(k, h), ys1.at[n], yr1.at[n])

    def yb(k, h):
        n = index[k, h]
        ring_b(("y", n), bterm(k, h), ysb.at[n], yrb.at[n], yhold.at[n])

    def yc(k, h):
        ring_c(bterm(k, h), yown.at[index[k, h]])

    def ym(k, h):
        n = index[k, h]
        ring_mid(("y", n), ys2.at[n], yr1.at[n], yr2.at[n], yhold.at[n])

    def ye(k, h):
        n = index[k, h]
        left, right = ring_end(("y", n), yrb.at[n], yr2.at[n], yown.at[n])
        finish(k, h, left, right)

    def ad(k):
        for h in range(2):
            for copy in st["g", k, h]:
                copy.wait_recv()
        if k < 3:
            adam_fetch(k + 1)
        row = lax.broadcasted_iota(jnp.int32, (128, 120), 0)
        col = lax.broadcasted_iota(jnp.int32, (128, 120), 1)
        pick = jnp.where(col == (row % 16) * 8 + row // 16, 1.0, 0.0).astype(bf16)
        for b in range(8):
            for i in range(3):
                st["m", k, b, i].wait()
            g = grad[:, b * 512 + k * 128:b * 512 + (k + 1) * 128]
            m = adam[k % 2, 0, b]
            one = beta_one * adam[k % 2, 1, b] + (1.0 - beta_one) * g
            two = beta_two * adam[k % 2, 2, b] + (1.0 - beta_two) * g * g
            one_hat = one / (1.0 - beta_one**bias_steps)
            two_hat = two / (1.0 - beta_two**bias_steps)
            new = m - learn_rate * (one_hat / (jnp.sqrt(two_hat) + adam_eps) + decay_rate * m)
            p = jnp.dot(pick, new.astype(bf16), preferred_element_type=f32).astype(bf16)
            wsend[k, :, :, b * 128:(b + 1) * 128] = p.reshape(8, 16, 128)
        st["l", k] = local(wsend.at[k, mp], wbuf.at[k, mp, slot])
        st["a", k] = []
        for (px, py), device in zip(peers, peer_place):
            st["a", k].append(send(wsend.at[k, px * 2 + py], wbuf.at[k, mp, slot], device))

    def ga(k):
        st["l", k].wait()
        for copy in st["a", k]:
            copy.wait_recv()
        mine = wbuf.at[k, :, slot]
        st["u", k] = send(mine, mine, z_up)
        st["d", k] = send(mine, mine, z_down)
        st["s", k] = [send(mine, mine, sib)]

    def gb(k):
        below, above = ((z + 3) % 4) * 2 + core, ((z + 1) % 4) * 2 + core
        st["u", k].wait_recv()
        low = wbuf.at[k, pl.ds(0, 4), below]
        st["ru", k] = send(low, low, z_up)
        st["d", k].wait_recv()
        high = wbuf.at[k, pl.ds(4, 4), above]
        st["rd", k] = send(high, high, z_down)
        for s in (below, above):
            st["s", k].append(send(wbuf.at[k, :, s], wbuf.at[k, :, s], sib))

    def gc(k):
        far = ((z + 2) % 4) * 2 + core
        st["ru", k].wait_recv()
        st["rd", k].wait_recv()
        st["s", k].append(send(wbuf.at[k, :, far], wbuf.at[k, :, far], sib))

    def mm(k):
        for copy in st["s", k]:
            copy.wait_recv()
        if "swap" not in st:
            st["sw"].wait_recv()
            st["swap"] = True
        lhs = abuf[...].reshape(384, 1024)

        def body(n, carry):
            cols = pl.ds(pl.multiple_of(n * 256, 256), 256)
            rhs = wbuf[k, :, :, :, cols].reshape(1024, 256)
            p = jnp.dot(lhs, rhs, preferred_element_type=f32).astype(bf16)
            for i in range(4):
                piece = p[(i % 2) * 192:(i % 2 + 1) * 192, (i // 2) * 128:(i // 2 + 1) * 128]
                part[k, 0, n, i] = piece[:96]
                part[k, 1, i, n] = piece[96:]
            return carry

        lax.fori_loop(0, 4, body, 0)
        lo, hi = pl.ds(0, 2), pl.ds(2, 2)
        for d, (me, up, down) in enumerate(axes):
            far, above, below = (me + 2) % 4, (me + 1) % 4, (me + 3) % 4
            st["f1", k, d] = [send(part.at[k, d, far, lo], r1.at[k, d, 0], up),
                              send(part.at[k, d, far, hi], r1.at[k, d, 1], down)]
            st["fb", k, d] = [send(part.at[k, d, above, hi], rb.at[k, d, 0], up),
                              send(part.at[k, d, below, lo], rb.at[k, d, 1], down)]

    def f2(k):
        for d, (me, up, down) in enumerate(axes):
            above, below = (me + 1) % 4, (me + 3) % 4
            st["f1", k, d][0].wait_recv()
            s2[k, d, 0] = (part[k, d, above, pl.ds(0, 2)].astype(f32) + r1[k, d, 0].astype(f32)).astype(bf16)
            first_half = send(s2.at[k, d, 0], r2.at[k, d, 0], up)
            st["f1", k, d][1].wait_recv()
            s2[k, d, 1] = (part[k, d, below, pl.ds(2, 2)].astype(f32) + r1[k, d, 1].astype(f32)).astype(bf16)
            st["f2", k, d] = [first_half, send(s2.at[k, d, 1], r2.at[k, d, 1], down)]

    def f3(k):
        for d, (me, up, down) in enumerate(axes):
            st["fb", k, d][1].wait_recv()
            st["f2", k, d][0].wait_recv()
            q[k, d, pl.ds(0, 2)] = (part[k, d, me, pl.ds(0, 2)].astype(f32) + rb[k, d, 1].astype(f32)
                                    + r2[k, d, 0].astype(f32)).astype(bf16)
            st["fb", k, d][0].wait_recv()
            st["f2", k, d][1].wait_recv()
            q[k, d, pl.ds(2, 2)] = (part[k, d, me, pl.ds(2, 2)].astype(f32) + rb[k, d, 0].astype(f32)
                                    + r2[k, d, 1].astype(f32)).astype(bf16)
            along, devices = (y, y_place) if d == 0 else (x, x_place)
            st["g", k, d] = [send(q.at[k, d, (along + i) % 4], ug.at[k, d, i - 1], devices[i - 1]) for i in range(1, 4)]

    def f5(k):
        cols = pl.ds(k * 128, 128)
        for d in range(2):
            lines = pl.ds(d * 96, 96)
            total = q[k, d, y if d == 0 else x].astype(f32)
            for i in range(3):
                st["g", k, d][i].wait_recv()
                total = total + ug[k, d, i].astype(f32)
            attended = att[pl.ds(2 * d, 2), k].reshape(96, 128).astype(bf16).astype(f32)
            stream = (residual[lines, cols].astype(f32) + attended).astype(bf16)
            out[lines, cols] = (stream.astype(f32) + total).astype(bf16)

    def ap():
        for g in range(HEADS // KV_HEADS):
            qbuf[:, g] = queries[:, :, g * 128:(g + 1) * 128].astype(f32)
        nbuf[0] = keys_new[...].astype(f32)
        nbuf[1] = values_new[...].astype(f32)

    def at(i):
        for copy in st["kv", i]:
            copy.wait()
        if i < 5:
            cache_fetch(i + 1)
        position = lax.broadcasted_iota(jnp.int32, (16, 128), 1)
        when = lax.broadcasted_iota(jnp.int32, (16, 1), 0) // 4
        heads = HEADS // KV_HEADS

        def rows(n, carry):
            for j in range(4):
                r = i * 8 + n * 4 + j
                qr = jnp.concatenate(
                    [qbuf[t, g, pl.ds(r, 1), :] for t in range(4) for g in range(heads)], axis=0)
                cached = lax.dot_general(qr.astype(bf16), kbuf[i % 2, n * 4 + j], (((1,), (1,)), ((), ())),
                                         preferred_element_type=f32) * HEAD_DIM ** (-0.5)
                cached = jnp.where(position < lengths[r], cached, -jnp.inf)
                fresh = []
                for s in range(4):
                    score = jnp.sum(qr * nbuf[0, s, pl.ds(r, 1), :], axis=1, keepdims=True) * HEAD_DIM ** (-0.5)
                    fresh.append(jnp.where(when >= s, score, -jnp.inf))
                highest = jnp.max(cached, axis=1, keepdims=True)
                for score in fresh:
                    highest = jnp.maximum(highest, score)
                cached = jnp.exp(cached - highest)
                fresh = [jnp.exp(score - highest) for score in fresh]
                total = jnp.sum(cached, axis=1, keepdims=True) + (fresh[0] + fresh[1]) + (fresh[2] + fresh[3])
                result = jnp.dot((cached / total).astype(bf16), vbuf[i % 2, n * 4 + j], preferred_element_type=f32)
                for s in range(4):
                    weight = (fresh[s] / total).astype(bf16).astype(f32)
                    result = result + weight * nbuf[1, s, pl.ds(r, 1), :]
                for t in range(4):
                    for g in range(heads):
                        att[t, g, pl.ds(r, 1), :] = result[t * heads + g:t * heads + g + 1]
            return carry

        lax.fori_loop(0, 2, rows, 0)

    steps = {"za": za, "zb": zb_, "zc": zc, "zm": zm_, "ze": ze, "zf": zf_, "hf": hf, "bs": bs, "bf": bf, "ya": ya,
             "yb": yb, "yc": yc, "ym": ym, "ye": ye, "ad": ad, "ga": ga, "gb": gb, "gc": gc, "mm": mm, "f2": f2,
             "f3": f3, "f5": f5, "ac": ac, "sw": sw, "ap": ap, "at": at}
    for name, *where in ORDER:
        steps[name](*where)
    for copy in sends:
        copy.wait_send()


def fused(learn_hidden, out_cot, acts, queries, keys, values, keys_new, values_new, lengths, residual, master, first, second):
    kinds = [a for pair in KIND for a in pair]
    nz, ny = max(kinds.count("Z"), 1), max(kinds.count("B"), 1)

    def ring(n, r):
        return [pltpu.VMEM((n, 2, r, 128), bf16)] * 7 + [pltpu.VMEM((n, r, 256), f32)]

    copies = 12 + 16 + 1 + 8 * 11 + 4 * 33
    locals_ = 4 + 16 + 12 + 4 * (24 + 1)
    return pl.pallas_call(
        fused_kernel,
        out_shape=(jax.ShapeDtypeStruct((192, 512), bf16), jax.ShapeDtypeStruct((120, 4096), f32)),
        in_specs=[pl.BlockSpec(memory_space=pl.ANY)] * 2 + [pl.BlockSpec(memory_space=pltpu.VMEM)] * 2
        + [pl.BlockSpec(memory_space=pl.ANY)] * 2 + [pl.BlockSpec(memory_space=pltpu.VMEM)] * 2
        + [pl.BlockSpec(memory_space=pltpu.SMEM), pl.BlockSpec(memory_space=pltpu.VMEM)]
        + [pl.BlockSpec(memory_space=pl.ANY)] * 3,
        out_specs=(pl.BlockSpec(memory_space=pltpu.VMEM),) * 2,
        scratch_shapes=[
            pltpu.VMEM((8, 240, 1024), bf16),
            pltpu.VMEM((4, 2, 1024, 256), bf16),
            *ring(nz, 480),
            pltpu.VMEM((nz, 240, 256), bf16),
            pltpu.VMEM((nz, 240, 256), bf16),
            pltpu.VMEM((512, 1920), bf16),
            pltpu.VMEM((4, 240, 1024), bf16),
            pltpu.VMEM((ny, 1024, 256), bf16),
            *ring(ny, 240),
            pltpu.VMEM((2, 2, 2, 2, 120, 128), f32),
            pltpu.VMEM((2, 3, 8, 120, 128), f32),
            pltpu.VMEM((4, 8, 16, 1024), bf16),
            pltpu.VMEM((4, 8, 8, 16, 1024), bf16),
            pltpu.VMEM((2, 192, 1024), bf16),
            pltpu.VMEM((2, 192, 1024), bf16),
            pltpu.VMEM((4, 2, 4, 4, 96, 128), bf16),
            *[pltpu.VMEM((4, 2, 2, 2, 96, 128), bf16)] * 4,
            pltpu.VMEM((4, 2, 4, 96, 128), bf16),
            pltpu.VMEM((4, 2, 3, 96, 128), bf16),
            pltpu.VMEM((2, 8, 128, 128), bf16),
            pltpu.VMEM((2, 8, 128, 128), bf16),
            pltpu.VMEM((4, 4, 48, 128), f32),
            pltpu.VMEM((2, 4, 48, 128), f32),
            pltpu.VMEM((4, 4, 48, 128), f32),
            pltpu.SemaphoreType.DMA((locals_,)),
            pltpu.SemaphoreType.DMA((copies,)),
            pltpu.SemaphoreType.DMA((copies,)),
        ],
        compiler_params=pltpu.CompilerParams(collective_id=0, has_side_effects=True, vmem_limit_bytes=54 * 2**20),
        cost_estimate=pl.CostEstimate(flops=11274289152, bytes_accessed=20 * 2**20, transcendentals=0),
        name="fused",
    )(learn_hidden, out_cot, acts, queries, keys, values, keys_new, values_new, lengths, residual, master, first, second)


def local(
    learn_hidden,
    out_cot,
    master,
    moment_one,
    moment_two,
    queries,
    keys_cache,
    values_cache,
    keys_new,
    values_new,
    lengths,
    residual,
    unit_acts,
):
    mixed, gradient_rows = fused(
        learn_hidden, out_cot, unit_acts.reshape(192, 1920), queries, keys_cache, values_cache, keys_new, values_new,
        lengths, residual.reshape(192, 512), master, moment_one, moment_two
    )
    mixed = mixed.reshape(residual.shape)
    moment_one_next = beta_one * moment_one + (1.0 - beta_one) * gradient_rows
    moment_two_next = beta_two * moment_two + (1.0 - beta_two) * gradient_rows * gradient_rows
    first_hat = moment_one_next / (1.0 - beta_one**bias_steps)
    second_hat = moment_two_next / (1.0 - beta_two**bias_steps)
    master_next = master - learn_rate * (
        first_hat / (jnp.sqrt(second_hat) + adam_eps) + decay_rate * master
    )
    return (mixed, master_next, moment_one_next, moment_two_next)


def solution(mesh):
    placed = (
        P("dp", "mp"),
        P("dp", None),
        P(("mp", "dp"), None),
        P(("mp", "dp"), None),
        P(("mp", "dp"), None),
        P(None, "dp", "mp"),
        P("dp", None, "mp"),
        P("dp", None, "mp"),
        P(None, "dp", "mp"),
        P(None, "dp", "mp"),
        P("dp"),
        P(None, "dp", "mp"),
        P(None, "dp", "mp", None),
    )
    return jax.shard_map(
        local,
        mesh=mesh,
        in_specs=placed,
        out_specs=(
            P(None, "dp", "mp"),
            P(("mp", "dp"), None),
            P(("mp", "dp"), None),
            P(("mp", "dp"), None),
        ),
        check_vma=False,
    )
```

```python
import functools
import jax
import jax.numpy as jnp
from jax import lax
from jax.experimental import pallas as pl
from jax.experimental.pallas import tpu as pltpu
from jax.sharding import PartitionSpec as P

MESHID = pl.DeviceIdType.MESH
bf16, f32 = jnp.bfloat16, jnp.float32
HEADS = 32
KV_HEADS = 8
HEAD_DIM = 128
CHUNKS = 4
KIND = (("Z", "B"), ("Z", "B"), ("B", "B"), ("B", "B"))
NEAR = (0, 0, 64, 128, 256, 256)
ORDER = [
    ("bs", 1, 1), ("za", 1, 0), ("bs", 0, 1), ("zb", 1, 0), ("za", 0, 0), ("ac",), ("bs", 2, 0), ("bf", 1, 1),
    ("zb", 0, 0), ("ap",), ("at", 0), ("hf", 0), ("zm", 0, 0), ("zc", 1, 0), ("zc", 0, 0), ("zm", 1, 0), ("bs", 2, 1),
    ("bs", 3, 1), ("at", 1), ("bf", 0, 1), ("hf", 1), ("at", 2), ("at", 3), ("hf", 2), ("ya", 1, 1), ("ze", 0, 0),
    ("ya", 0, 1), ("yb", 0, 1), ("bf", 2, 0), ("hf", 3), ("yb", 1, 1), ("ym", 0, 1), ("bs", 3, 0), ("bf", 2, 1),
    ("yc", 1, 1), ("ze", 1, 0), ("ym", 1, 1), ("yc", 0, 1), ("ya", 2, 0), ("bf", 3, 1), ("yb", 2, 0), ("ya", 2, 1),
    ("yb", 2, 1), ("zf", 0, 0), ("ye", 0, 1), ("yc", 2, 1), ("ym", 2, 0), ("bf", 3, 0), ("ya", 3, 1), ("ym", 2, 1),
    ("yb", 3, 1), ("ad", 0), ("ya", 3, 0), ("yb", 3, 0), ("ye", 1, 1), ("ym", 3, 1), ("yc", 3, 1), ("yc", 2, 0),
    ("zf", 1, 0), ("ga", 0), ("ye", 2, 0), ("ye", 2, 1), ("ad", 1), ("ad", 2), ("ye", 3, 1), ("yc", 3, 0),
    ("ym", 3, 0), ("ga", 1), ("sw",), ("gb", 0), ("ye", 3, 0), ("at", 4), ("ga", 2), ("ad", 3), ("gc", 0), ("gb", 1),
    ("mm", 0), ("at", 5), ("ga", 3), ("gc", 1), ("gb", 2), ("mm", 1), ("f3", 0), ("gb", 3), ("gc", 2), ("f3", 1),
    ("mm", 2), ("gc", 3), ("f5", 0), ("mm", 3), ("f3", 2), ("f3", 3), ("f5", 2), ("f5", 1), ("f5", 3),
]
beta_one = 0.9
beta_two = 0.999
learn_rate = 0.01
decay_rate = 0.1
adam_eps = 1e-08
bias_steps = 10.0


def coords():
    dp, mp = lax.axis_index("dp"), lax.axis_index("mp")
    return dp // 4, (dp // 2) % 2, dp % 2, mp // 2, mp % 2


def place(z, y_lo, core, x, y_hi):
    return ((z * 2 + y_lo) * 2 + core, x * 2 + y_hi)


def fused_kernel(hidden_in, cot, acts, queries, keys, values, keys_new, values_new, lengths, residual,
                 master, first, second, out, grad_out,
                 hs, cs, zs1, zsb, zs2, zr1, zrb, zr2, zhold, zown, zys, zyr,
                 hraw, ho, co, ys1, ysb, ys2, yr1, yrb, yr2, yhold, yown, gbuf, grad, adam,
                 wsend, wbuf, asend, abuf, part, r1, q, ug, kbuf, vbuf, qbuf, nbuf, att,
                 loc_sem, send_sem, recv_sem):
    z, y_lo, core, x, y_hi = coords()
    y, mp, slot = y_hi * 2 + y_lo, x * 2 + y_hi, z * 2 + core

    def at_y(yy):
        return place(z, yy % 2, core, x, yy // 2)

    sib = place(z, y_lo, 1 - core, x, y_hi)
    z_up, z_down = place((z + 1) % 4, y_lo, core, x, y_hi), place((z + 3) % 4, y_lo, core, x, y_hi)
    y_place = [at_y((y + d) % 4) for d in range(1, 4)]
    x_place = [place(z, y_lo, core, (x + d) % 4, y_hi) for d in range(1, 4)]
    axes = ((x, x_place), (y, y_place))
    across = place(z, 1 - y_lo, core, x, y_hi)
    peers = [((x + i // 2) % 4, (y_hi + i % 2) % 2) for i in range(1, 8)]
    peer_place = [place(z, y_lo, core, px, py) for px, py in peers]

    count = [0, 0]
    sends = []
    st = {}

    def send(src, dst, device):
        i = count[0]
        count[0] += 1
        copy = pltpu.make_async_remote_copy(
            src_ref=src, dst_ref=dst, send_sem=send_sem.at[i], recv_sem=recv_sem.at[i],
            device_id=device, device_id_type=MESHID)
        copy.start()
        sends.append(copy)
        return copy

    def local(src, dst):
        i = count[1]
        count[1] += 1
        copy = pltpu.make_async_copy(src, dst, loc_sem.at[i])
        copy.start()
        return copy

    other = at_y((y + 3 + 2 * y_lo) % 4)
    raw = local(hidden_in, hraw)
    barrier = pltpu.get_barrier_semaphore()
    everyone = peer_place + [sib, z_up, z_down, y_place[0], y_place[2]]
    for device in everyone:
        pl.semaphore_signal(barrier, inc=1, device_id=device, device_id_type=MESHID)
    zp, zm, zf = (z + 1) % 4, (z + 3) % 4, (z + 2) % 4
    offset = [2, 1, 3, 0]

    def turn_hidden(i):
        row = lax.broadcasted_iota(jnp.int32, (240, 384), 0)
        lane = lax.broadcasted_iota(jnp.int32, (240, 384), 1)
        for yl in range(2):
            b = ((z + offset[i]) % 4) * 2 + yl
            start = jnp.minimum(b * 240 // 128 * 128, 1536)
            e = jnp.where(lane - (b * 240 - start) == row, 1.0, 0.0).astype(bf16)
            window = hraw[:, pl.ds(pl.multiple_of(start, 128), 384)]
            turned = lax.dot_general(e, window, (((1,), (1,)), ((), ())), preferred_element_type=f32)
            hs[b, :, pl.ds(0, 512)] = turned.astype(bf16)

    def share_hidden(i):
        zb = (z + offset[i]) % 4
        blocks = pl.ds(zb * 2, 2)
        st["h", i] = send(hs.at[blocks, :, pl.ds(0, 512)], hs.at[blocks, :, pl.ds(512, 512)], sib)
        st["hy", i] = send(hs.at[zb * 2 + 1 - y_lo, :, pl.ds(0, 512)], ho.at[i, :, pl.ds(0, 512)], across)

    def hf(i):
        st["hy", i].wait_recv()
        st["hs", i] = send(ho.at[i, :, pl.ds(0, 512)], ho.at[i, :, pl.ds(512, 512)], sib)

    def share_cotangent(k, h):
        st["c", k, h] = []
        for i in range(2):
            mine = pl.ds(pl.multiple_of((4 * core + 2 * h + i) * 512 + k * 128, 128), 128)
            theirs = pl.ds(pl.multiple_of((4 - 4 * core + 2 * h + i) * 512 + k * 128, 128), 128)
            lanes = pl.ds(i * 128, 128)
            st["c", k, h].append(send(cot.at[:, theirs], cs.at[k, h, pl.ds(512, 512), lanes], sib))
            st["c", k, h].append(local(cot.at[:, mine], cs.at[k, h, pl.ds(0, 512), lanes]))

    first_use = [where for name, *where in ORDER if name in ("bs", "za")]
    raw.wait()
    turn_hidden(0)
    pl.semaphore_wait(barrier, len(everyone))
    share_hidden(0)
    share_cotangent(*first_use[0])
    for i in range(1, 4):
        turn_hidden(i)
        share_hidden(i)
    for where in first_use[1:]:
        share_cotangent(*where)

    def cache_fetch(i):
        rows = pl.ds(i * 8, 8)
        st["kv", i] = [local(keys.at[rows], kbuf.at[i % 2]), local(values.at[rows], vbuf.at[i % 2])]

    cache_fetch(0)

    def hidden(i):
        if ("got", i) not in st:
            st["got", i] = True
            st["h", i].wait_recv()

    def adam_fetch(k):
        for b in range(8):
            for i, ref in enumerate((master, first, second)):
                st["m", k, b, i] = local(ref.at[:, pl.ds(b * 512 + k * 128, 128)], adam.at[k % 2, i, b])

    adam_fetch(0)

    def ac():
        unit = lax.broadcasted_iota(jnp.int32, (384, 256), 0)
        lane = lax.broadcasted_iota(jnp.int32, (384, 256), 1)
        owner = (lane % 128) // 16
        target = ((owner // 2) * 4 + (lane // 128) * 2 + owner % 2) * 15 + lane % 16
        target = jnp.where(lane % 16 < 15, target, -1000)
        for b in range(8):
            start, shift = (b * 240) // 128 * 128, (b * 240) % 128
            depth = 256 if shift + 240 <= 256 else 384
            e = jnp.where(unit[:depth] - shift == target[:depth], 1.0, 0.0).astype(bf16)
            a = jnp.dot(acts[:, start:start + depth], e, preferred_element_type=f32).astype(bf16)
            asend[0, :, b * 128:(b + 1) * 128] = a[:, :128]
            asend[1, :, b * 128:(b + 1) * 128] = a[:, 128:]
        abuf[y_lo] = asend[y_lo]

    def sw():
        st["sw"] = send(asend.at[1 - y_lo], abuf.at[y_lo], across)

    def ready(k, h):
        for i in range(2):
            st["c", k, h][2 * i].wait_recv()
            st["c", k, h][2 * i + 1].wait()

    def ring_a(key, term, s1, r1):
        hidden(0)
        p = term(0, zf)
        s1[0] = p[:, :128].astype(bf16)
        s1[1] = p[:, 128:].astype(bf16)
        st["r1", key] = [send(s1.at[0], r1.at[0], z_up), send(s1.at[1], r1.at[1], z_down)]

    def ring_b(key, term, sb, rb, hold):
        hidden(1)
        p = term(1, zp)
        sb[0] = p[:, 128:].astype(bf16)
        b0 = send(sb.at[0], rb.at[0], z_up)
        hold[0] = p[:, :128].astype(hold.dtype)
        hidden(2)
        p = term(2, zm)
        sb[1] = p[:, :128].astype(bf16)
        b1 = send(sb.at[1], rb.at[1], z_down)
        hold[1] = p[:, 128:].astype(hold.dtype)
        st["rb", key] = [b0, b1]

    def ring_c(term, own):
        hidden(3)
        own[...] = term(3, z)

    def ring_mid(key, s2, r1, r2, hold):
        st["r2", key] = []
        for d, device in ((0, z_up), (1, z_down)):
            st["r1", key][d].wait_recv()
            s2[d] = (hold[d].astype(f32) + r1[d].astype(f32)).astype(bf16)
            st["r2", key].append(send(s2.at[d], r2.at[d], device))

    def ring_end(key, rb, r2, own):
        st["rb", key][1].wait_recv()
        st["r2", key][0].wait_recv()
        left = own[:, :128] + rb[1].astype(f32) + r2[0].astype(f32)
        st["rb", key][0].wait_recv()
        st["r2", key][1].wait_recv()
        right = own[:, 128:] + rb[0].astype(f32) + r2[1].astype(f32)
        return left, right

    def finish(k, h, left, right):
        for copy in st.get(("g", k - 2, h), []):
            copy.wait_send()
            sends[:] = [c for c in sends if c is not copy]
        st["g", k, h] = []
        for i, half in enumerate((left, right)):
            gbuf[k % 2, h, i] = half.reshape(2, 120, 128)
            cols = pl.ds(pl.multiple_of((4 * core + 2 * h + i) * 512 + k * 128, 128), 128)
            st["g", k, h].append(send(gbuf.at[k % 2, h, i, 1 - core], grad.at[:, cols], sib))
            grad[:, cols] = gbuf[k % 2, h, i, core]

    numbers = {"Z": 0, "B": 0}
    index = {}
    for k in range(4):
        for h in range(2):
            index[k, h] = numbers[KIND[k][h]]
            numbers[KIND[k][h]] += 1

    def zterm(k, h):
        def term(i, zb):
            return jnp.dot(hs[pl.ds(2 * zb, 2)].reshape(480, 1024), cs[k, h], preferred_element_type=f32)

        return term

    def za(k, h):
        n = index[k, h]
        ready(k, h)
        ring_a(("z", n), zterm(k, h), zs1.at[n], zr1.at[n])

    def zb_(k, h):
        n = index[k, h]
        ring_b(("z", n), zterm(k, h), zsb.at[n], zrb.at[n], zhold.at[n])

    def zc(k, h):
        ring_c(zterm(k, h), zown.at[index[k, h]])

    def zm_(k, h):
        n = index[k, h]
        ring_mid(("z", n), zs2.at[n], zr1.at[n], zr2.at[n], zhold.at[n])

    def ze(k, h):
        n = index[k, h]
        left, right = ring_end(("z", n), zrb.at[n], zr2.at[n], zown.at[n])
        zown[n, :, pl.ds(0, 128)] = left
        zown[n, :, pl.ds(128, 128)] = right
        theirs = pl.ds(pl.multiple_of((1 - y_lo) * 240, 16), 240)
        zys[n] = zown[n, theirs, :].astype(bf16)
        st["zy", n] = send(zys.at[n], zyr.at[n], across)

    def zf_(k, h):
        n = index[k, h]
        st["zy", n].wait_recv()
        mine = pl.ds(pl.multiple_of(y_lo * 240, 16), 240)
        total = zown[n, mine, :] + zyr[n].astype(f32)
        finish(k, h, total[:, :128], total[:, 128:])

    def bs(k, h):
        n = index[k, h]
        ready(k, h)
        base = (x % 2) * 512
        few = NEAR[n]
        rest = pl.ds(pl.multiple_of(base + few, 16), 512 - few)
        st["by", n] = [send(cs.at[k, h, rest], co.at[n, rest], other)]
        if few > 0:
            near = pl.ds(pl.multiple_of(base, 16), few)
            st["by", n].append(send(cs.at[k, h, near], co.at[n, near], across))

    def bf(k, h):
        n = index[k, h]
        for copy in st["by", n]:
            copy.wait_recv()
        base = (x % 2) * 512
        low, high = pl.ds(pl.multiple_of(base, 16), 256), pl.ds(pl.multiple_of(base + 256, 16), 256)
        st["bx", n] = [send(co.at[n, low], co.at[n, low], x_place[0]), send(co.at[n, high], co.at[n, high], x_place[2])]

    def bterm(k, h):
        n = index[k, h]

        def term(i, zb):
            if ("far", i) not in st:
                st["far", i] = True
                st["hs", i].wait_recv()
            return (jnp.dot(hs[2 * zb + y_lo], cs[k, h], preferred_element_type=f32)
                    + jnp.dot(ho[i], co[n], preferred_element_type=f32))

        return term

    def ya(k, h):
        n = index[k, h]
        for copy in st["bx", n]:
            copy.wait_recv()
        ring_a(("y", n), bterm(k, h), ys1.at[n], yr1.at[n])

    def yb(k, h):
        n = index[k, h]
        ring_b(("y", n), bterm(k, h), ysb.at[n], yrb.at[n], yhold.at[n])

    def yc(k, h):
        ring_c(bterm(k, h), yown.at[index[k, h]])

    def ym(k, h):
        n = index[k, h]
        ring_mid(("y", n), ys2.at[n], yr1.at[n], yr2.at[n], yhold.at[n])

    def ye(k, h):
        n = index[k, h]
        left, right = ring_end(("y", n), yrb.at[n], yr2.at[n], yown.at[n])
        finish(k, h, left, right)

    def ad(k):
        for h in range(2):
            for copy in st["g", k, h]:
                copy.wait_recv()
        st["o", k] = []
        for b in range(8):
            cols = pl.ds(b * 512 + k * 128, 128)
            st["o", k].append(local(grad.at[:, cols], grad_out.at[:, cols]))
        if k < 3:
            adam_fetch(k + 1)
        row = lax.broadcasted_iota(jnp.int32, (128, 120), 0)
        col = lax.broadcasted_iota(jnp.int32, (128, 120), 1)
        pick = jnp.where(col == (row % 16) * 8 + row // 16, 1.0, 0.0).astype(bf16)
        for b in range(8):
            for i in range(3):
                st["m", k, b, i].wait()
            g = grad[:, b * 512 + k * 128:b * 512 + (k + 1) * 128]
            m = adam[k % 2, 0, b]
            one = beta_one * adam[k % 2, 1, b] + (1.0 - beta_one) * g
            two = beta_two * adam[k % 2, 2, b] + (1.0 - beta_two) * g * g
            one_hat = one / (1.0 - beta_one**bias_steps)
            two_hat = two / (1.0 - beta_two**bias_steps)
            new = m - learn_rate * (one_hat / (jnp.sqrt(two_hat) + adam_eps) + decay_rate * m)
            p = jnp.dot(pick, new.astype(bf16), preferred_element_type=f32).astype(bf16)
            wsend[k, :, :, b * 128:(b + 1) * 128] = p.reshape(8, 16, 128)
        st["l", k] = local(wsend.at[k, mp], wbuf.at[k, mp, slot])
        st["a", k] = []
        for (px, py), device in zip(peers, peer_place):
            st["a", k].append(send(wsend.at[k, px * 2 + py], wbuf.at[k, mp, slot], device))

    def ga(k):
        st["l", k].wait()
        for copy in st["a", k]:
            copy.wait_recv()
        mine = wbuf.at[k, :, slot]
        st["u", k] = send(mine, mine, z_up)
        st["d", k] = send(mine, mine, z_down)
        st["s", k] = [send(mine, mine, sib)]

    def gb(k):
        below, above = ((z + 3) % 4) * 2 + core, ((z + 1) % 4) * 2 + core
        st["u", k].wait_recv()
        low = wbuf.at[k, pl.ds(0, 4), below]
        st["ru", k] = send(low, low, z_up)
        st["d", k].wait_recv()
        high = wbuf.at[k, pl.ds(4, 4), above]
        st["rd", k] = send(high, high, z_down)
        for s in (below, above):
            st["s", k].append(send(wbuf.at[k, :, s], wbuf.at[k, :, s], sib))

    def gc(k):
        far = ((z + 2) % 4) * 2 + core
        st["ru", k].wait_recv()
        st["rd", k].wait_recv()
        st["s", k].append(send(wbuf.at[k, :, far], wbuf.at[k, :, far], sib))

    def mm(k):
        for copy in st["s", k]:
            copy.wait_recv()
        if "swap" not in st:
            st["sw"].wait_recv()
            st["swap"] = True
        lhs = abuf[...].reshape(384, 1024)

        def body(n, carry):
            cols = pl.ds(pl.multiple_of(n * 256, 256), 256)
            rhs = wbuf[k, :, :, :, cols].reshape(1024, 256)
            p = jnp.dot(lhs, rhs, preferred_element_type=f32).astype(bf16)
            for i in range(4):
                piece = p[(i % 2) * 192:(i % 2 + 1) * 192, (i // 2) * 128:(i // 2 + 1) * 128]
                part[k, 0, n, i] = piece[:96]
                part[k, 1, i, n] = piece[96:]
            return carry

        lax.fori_loop(0, 4, body, 0)
        for d, (me, devices) in enumerate(axes):
            st["f1", k, d] = [send(part.at[k, d, (me + i) % 4], r1.at[k, d, i - 1], devices[i - 1]) for i in range(1, 4)]

    def f3(k):
        for d, (me, _) in enumerate(axes):
            total = part[k, d, me].astype(f32)
            for i in range(3):
                st["f1", k, d][i].wait_recv()
                total = total + r1[k, d, i].astype(f32)
            q[k, d] = total.astype(bf16)
            along, devices = (y, y_place) if d == 0 else (x, x_place)
            st["g", k, d] = [send(q.at[k, d, (along + i) % 4], ug.at[k, d, i - 1], devices[i - 1]) for i in range(1, 4)]

    def f5(k):
        cols = pl.ds(k * 128, 128)
        for d in range(2):
            lines = pl.ds(d * 96, 96)
            total = q[k, d, y if d == 0 else x].astype(f32)
            for i in range(3):
                st["g", k, d][i].wait_recv()
                total = total + ug[k, d, i].astype(f32)
            attended = att[pl.ds(2 * d, 2), k].reshape(96, 128).astype(bf16).astype(f32)
            stream = (residual[lines, cols].astype(f32) + attended).astype(bf16)
            out[lines, cols] = (stream.astype(f32) + total).astype(bf16)

    def ap():
        for g in range(HEADS // KV_HEADS):
            qbuf[:, g] = queries[:, :, g * 128:(g + 1) * 128].astype(f32)
        nbuf[0] = keys_new[...].astype(f32)
        nbuf[1] = values_new[...].astype(f32)

    def at(i):
        for copy in st["kv", i]:
            copy.wait()
        if i < 5:
            cache_fetch(i + 1)
        lines = slice(i * 8, (i + 1) * 8)
        lane = lax.broadcasted_iota(jnp.int32, (128, 128), 1)
        line = lax.broadcasted_iota(jnp.int32, (128, 128), 0) % 8
        when = lax.broadcasted_iota(jnp.int32, (128, 1), 0) // 32
        asked = qbuf[:, :, lines, :].reshape(128, 128)
        asked_low = asked.astype(bf16)
        cached = jnp.zeros((128, 128), f32)
        limit = jnp.zeros((128, 128), jnp.int32)
        for j in range(8):
            scores = lax.dot_general(asked_low, kbuf[i % 2, j], (((1,), (1,)), ((), ())), preferred_element_type=f32)
            cached = jnp.where(line == j, scores, cached)
            limit = jnp.where(line == j, lengths[i * 8 + j], limit)
        cached = jnp.where(lane < limit, cached * HEAD_DIM ** (-0.5), -jnp.inf)
        highest = jnp.max(cached, axis=1, keepdims=True)
        fresh = []
        for s in range(4):
            product = asked.reshape(16, 8, 128) * nbuf[0, s, lines, :][None]
            score = jnp.sum(product.reshape(128, 128), axis=1, keepdims=True) * HEAD_DIM ** (-0.5)
            fresh.append(jnp.where(when >= s, score, -jnp.inf))
            highest = jnp.maximum(highest, fresh[s])
        cached = jnp.exp(cached - highest)
        fresh = [jnp.exp(score - highest) for score in fresh]
        total = jnp.sum(cached, axis=1, keepdims=True) + (fresh[0] + fresh[1]) + (fresh[2] + fresh[3])
        weights = (cached / total).astype(bf16)
        result = jnp.zeros((128, 128), f32)
        for j in range(8):
            sums = jnp.dot(weights, vbuf[i % 2, j], preferred_element_type=f32)
            result = jnp.where(line == j, sums, result)
        for s in range(4):
            weight = (fresh[s] / total).astype(bf16).astype(f32)
            value = jnp.broadcast_to(nbuf[1, s, lines, :][None], (16, 8, 128)).reshape(128, 128)
            result = result + weight * value
        att[:, :, lines, :] = result.reshape(4, 4, 8, 128)

    steps = {"za": za, "zb": zb_, "zc": zc, "zm": zm_, "ze": ze, "zf": zf_, "hf": hf, "bs": bs, "bf": bf, "ya": ya,
             "yb": yb, "yc": yc, "ym": ym, "ye": ye, "ad": ad, "ga": ga, "gb": gb, "gc": gc, "mm": mm,
             "f3": f3, "f5": f5, "ac": ac, "sw": sw, "ap": ap, "at": at}
    for name, *where in ORDER:
        steps[name](*where)
    for k in range(4):
        for copy in st["o", k]:
            copy.wait()
    for copy in sends:
        copy.wait_send()


def fused(learn_hidden, out_cot, acts, queries, keys, values, keys_new, values_new, lengths, residual, master, first, second):
    kinds = [a for pair in KIND for a in pair]
    nz, ny = max(kinds.count("Z"), 1), max(kinds.count("B"), 1)

    def ring(n, r):
        return [pltpu.VMEM((n, 2, r, 128), bf16)] * 7 + [pltpu.VMEM((n, r, 256), f32)]

    copies = 12 + 16 + 1 + 8 * 11 + 4 * 33
    locals_ = 4 + 16 + 12 + 4 * (32 + 1)
    return pl.pallas_call(
        fused_kernel,
        out_shape=(jax.ShapeDtypeStruct((192, 512), bf16), jax.ShapeDtypeStruct((120, 4096), f32)),
        in_specs=[pl.BlockSpec(memory_space=pl.ANY)] * 2 + [pl.BlockSpec(memory_space=pltpu.VMEM)] * 2
        + [pl.BlockSpec(memory_space=pl.ANY)] * 2 + [pl.BlockSpec(memory_space=pltpu.VMEM)] * 2
        + [pl.BlockSpec(memory_space=pltpu.SMEM), pl.BlockSpec(memory_space=pltpu.VMEM)]
        + [pl.BlockSpec(memory_space=pl.ANY)] * 3,
        out_specs=(pl.BlockSpec(memory_space=pltpu.VMEM), pl.BlockSpec(memory_space=pl.ANY)),
        scratch_shapes=[
            pltpu.VMEM((8, 240, 1024), bf16),
            pltpu.VMEM((4, 2, 1024, 256), bf16),
            *ring(nz, 480),
            pltpu.VMEM((nz, 240, 256), bf16),
            pltpu.VMEM((nz, 240, 256), bf16),
            pltpu.VMEM((512, 1920), bf16),
            pltpu.VMEM((4, 240, 1024), bf16),
            pltpu.VMEM((ny, 1024, 256), bf16),
            *ring(ny, 240),
            pltpu.VMEM((2, 2, 2, 2, 120, 128), f32),
            pltpu.VMEM((120, 4096), f32),
            pltpu.VMEM((2, 3, 8, 120, 128), f32),
            pltpu.VMEM((4, 8, 16, 1024), bf16),
            pltpu.VMEM((4, 8, 8, 16, 1024), bf16),
            pltpu.VMEM((2, 192, 1024), bf16),
            pltpu.VMEM((2, 192, 1024), bf16),
            pltpu.VMEM((4, 2, 4, 4, 96, 128), bf16),
            pltpu.VMEM((4, 2, 3, 4, 96, 128), bf16),
            pltpu.VMEM((4, 2, 4, 96, 128), bf16),
            pltpu.VMEM((4, 2, 3, 96, 128), bf16),
            pltpu.VMEM((2, 8, 128, 128), bf16),
            pltpu.VMEM((2, 8, 128, 128), bf16),
            pltpu.VMEM((4, 4, 48, 128), f32),
            pltpu.VMEM((2, 4, 48, 128), f32),
            pltpu.VMEM((4, 4, 48, 128), f32),
            pltpu.SemaphoreType.DMA((locals_,)),
            pltpu.SemaphoreType.DMA((copies,)),
            pltpu.SemaphoreType.DMA((copies,)),
        ],
        compiler_params=pltpu.CompilerParams(collective_id=0, has_side_effects=True, vmem_limit_bytes=54 * 2**20),
        cost_estimate=pl.CostEstimate(flops=11274289152, bytes_accessed=20 * 2**20, transcendentals=0),
        name="fused",
    )(learn_hidden, out_cot, acts, queries, keys, values, keys_new, values_new, lengths, residual, master, first, second)


def local(
    learn_hidden,
    out_cot,
    master,
    moment_one,
    moment_two,
    queries,
    keys_cache,
    values_cache,
    keys_new,
    values_new,
    lengths,
    residual,
    unit_acts,
):
    mixed, gradient_rows = fused(
        learn_hidden, out_cot, unit_acts.reshape(192, 1920), queries, keys_cache, values_cache, keys_new, values_new,
        lengths, residual.reshape(192, 512), master, moment_one, moment_two
    )
    mixed = mixed.reshape(residual.shape)
    moment_one_next = beta_one * moment_one + (1.0 - beta_one) * gradient_rows
    moment_two_next = beta_two * moment_two + (1.0 - beta_two) * gradient_rows * gradient_rows
    first_hat = moment_one_next / (1.0 - beta_one**bias_steps)
    second_hat = moment_two_next / (1.0 - beta_two**bias_steps)
    master_next = master - learn_rate * (
        first_hat / (jnp.sqrt(second_hat) + adam_eps) + decay_rate * master
    )
    return (mixed, master_next, moment_one_next, moment_two_next)


def solution(mesh):
    placed = (
        P("dp", "mp"),
        P("dp", None),
        P(("mp", "dp"), None),
        P(("mp", "dp"), None),
        P(("mp", "dp"), None),
        P(None, "dp", "mp"),
        P("dp", None, "mp"),
        P("dp", None, "mp"),
        P(None, "dp", "mp"),
        P(None, "dp", "mp"),
        P("dp"),
        P(None, "dp", "mp"),
        P(None, "dp", "mp", None),
    )
    return jax.shard_map(
        local,
        mesh=mesh,
        in_specs=placed,
        out_specs=(
            P(None, "dp", "mp"),
            P(("mp", "dp"), None),
            P(("mp", "dp"), None),
            P(("mp", "dp"), None),
        ),
        check_vma=False,
    )
```
